512 devices in a mesh: shot: 64 (over z, x, core), chan: 8 (over y).
Axes of the slice: x: 4, y: 8, z: 8, core: 2. Of those that a mesh axis runs over, the one named last changes fastest.
Arguments:
- blended: float32 [1024, 32, 1024], P('shot', 'chan'), may hold values from -40 to 40, as said below
- estimate: bfloat16 [1024, 32, 1024], P('shot', 'chan'), may hold values from -40 to 40, as said below
- neighbour_sources: int32 [1024, 6], P('shot'), may hold values from 0 to 1023, as said below
- partner_lags: int32 [1024, 6], P('shot'), may hold values from -1023 to 1024, as said below
- threshold_level: int32 [1], replicated, may hold values from 2 to 6
Outputs:
- deblended: float32 [1024, 32, 1024], P('shot', 'chan')
The draws below stay inside these ranges and needn't reach their ends.
Inputs may be any that keep to these rules, and one draw needn't show every extreme that they name: `neighbour_sources`: shot s is at position k of fleet g0, where (s + 1) modulo 1024 equals g0 * 512 + k. Slot 3 * g + e (e in 0, 1, 2) holds the shot at position k + e - 1 of fleet g, that is (g * 512 + k + e - 2) modulo 1024, when that position lies in 0..511, the shot is not s, and its window meets that of s; every other slot holds s itself. The relation is symmetric. `partner_lags`: A listed partner's offset is its firing time minus that of the shot, of magnitude under 1024, and the partner lists the shot with the negated offset; a slot holding the shot itself has offset 1024. `blended`: Real-valued traces. `estimate`: Real-valued traces.
All inputs are finite; a program needn't handle non-finite values.
Results may differ from the reference program's by a relative error of at most 0.02.
Values may be sent and summed in bfloat16 or wider, within the bound.
No kernel may reach another device: no remote copies, remote signals or barrier semaphores. Data moves between devices by JAX's collectives and lax.ppermute only.
A program may use at most 64 MiB of HBM per device.

```python
import math
import jax
import jax.numpy as jnp
from jax import lax

NT = 1024
MAXP = 6
NS = 1024
NC = 32
SPF = 512


def channel_gain(key, spread):
    jitter = jax.random.uniform(jax.random.fold_in(key, 101), (1, NC, 1), jnp.float32, 0.8, 1.25)
    position_ramp = lax.broadcasted_iota(jnp.float32, (1, NC, 1), 1) / max(NC - 1, 1)
    return jnp.exp(math.log(spread) * (position_ramp - 0.5)) * jitter


def source_emission_plan(key):
    shot_ids = lax.iota(jnp.int32, NS)
    line_ids = (shot_ids + 1) % NS
    fleet_ids = line_ids // SPF
    fleet_pos = line_ids % SPF
    dither = jax.random.randint(jax.random.fold_in(key, 202), (NS,), 0, NT // 2)
    fire_times = fleet_pos * (NT * 25 // 32) + dither
    slot_ids = lax.broadcasted_iota(jnp.int32, (NS, MAXP), 1)
    other_fleet = slot_ids // 3
    step_off = slot_ids % 3 - 1
    other_pos = fleet_pos[:, None] + step_off
    inside = (other_pos >= 0) & (other_pos < SPF)
    other_shot = (other_fleet * SPF + jnp.clip(other_pos, 0, SPF - 1) - 1 + NS) % NS
    time_gap = jnp.take(fire_times, other_shot) - fire_times[:, None]
    itself = (other_fleet == fleet_ids[:, None]) & (step_off == 0)
    meets = inside & jnp.logical_not(itself) & (jnp.abs(time_gap) < NT)
    partner_grid = jnp.where(meets, other_shot, shot_ids[:, None]).astype(jnp.int32)
    delay_operator_matrix = jnp.where(meets, time_gap, NT).astype(jnp.int32)
    return (partner_grid, delay_operator_matrix)


def draw_blended(key, part):
    gains = channel_gain(key, 10.0)
    key = jax.random.fold_in(key, 1)
    random_part = jax.random.truncated_normal(key, -4.0, 4.0, (NS, NC, NT), jnp.float32)
    trace_values = gains * random_part
    return trace_values.astype(jnp.float32)


def draw_estimate(key, part):
    gains = channel_gain(key, 10.0)
    key = jax.random.fold_in(key, 2)
    random_part = jax.random.truncated_normal(key, -4.0, 4.0, (NS, NC, NT), jnp.float32)
    trace_values = gains * random_part
    return trace_values.astype(jnp.bfloat16)


def draw_neighbour_sources(key, part):
    partner_grid, delay_operator_matrix = source_emission_plan(key)
    return partner_grid


def draw_partner_lags(key, part):
    partner_grid, delay_operator_matrix = source_emission_plan(key)
    return delay_operator_matrix


def setup_inputs(seed: int = 0) -> dict:
    splits = jax.random.split(jax.random.key(seed), 6)
    blended = draw_blended(jax.random.fold_in(splits[5], 71), 0)
    estimate = draw_estimate(jax.random.fold_in(splits[5], 71), 0)
    neighbour_sources = draw_neighbour_sources(jax.random.fold_in(splits[5], 71), 0)
    partner_lags = draw_partner_lags(jax.random.fold_in(splits[5], 71), 0)
    threshold_level = jax.random.randint(splits[4], (1,), 2, 7).astype(jnp.int32)
    return dict(blended=blended, estimate=estimate, neighbour_sources=neighbour_sources, partner_lags=partner_lags, threshold_level=threshold_level)


STEP_SIZE = 0.25
LEVEL_UNIT = 1.0 / 64.0


def lagged_recordings(traces, delays):
    length = traces.shape[2]
    padded = jnp.pad(traces, ((0, 0), (0, 0), (length, length)))

    def one_trace(single, sample_delay):
        return lax.dynamic_slice_in_dim(single, (length - sample_delay).astype(jnp.int32), length, 1)

    return jax.vmap(one_trace)(padded, delays)


def companion_sum(incoming_recordings, neighbour_sources, partner_lags):
    accumulated_total = jnp.zeros(incoming_recordings.shape, jnp.float32)
    for emission_position_number in range(neighbour_sources.shape[1]):
        collected_gather = jnp.take(incoming_recordings, neighbour_sources[:, emission_position_number], axis=0)
        accumulated_total = accumulated_total + lagged_recordings(collected_gather, partner_lags[:, emission_position_number]).astype(jnp.float32)
    return accumulated_total


def reference(blended, estimate, neighbour_sources, partner_lags, threshold_level):
    first_sum = companion_sum(estimate, neighbour_sources, partner_lags)
    residual = (blended - estimate.astype(jnp.float32) - first_sum).astype(jnp.bfloat16)
    second_sum = companion_sum(residual, neighbour_sources, partner_lags)
    updated = (estimate.astype(jnp.float32) + STEP_SIZE * (residual.astype(jnp.float32) + second_sum)).astype(jnp.bfloat16)
    samples = updated.shape[2]
    freq_count = samples // 2
    shot_count = updated.shape[0]
    fourier_spectrum = jnp.fft.fft(updated.astype(jnp.float32), axis=2)[:, :, :freq_count] * samples ** -0.5
    spec_real = jnp.real(fourier_spectrum).astype(jnp.bfloat16)
    spec_imag = jnp.imag(fourier_spectrum).astype(jnp.bfloat16)
    transform = jnp.fft.fft(lax.complex(spec_real.astype(jnp.float32), spec_imag.astype(jnp.float32)), axis=0) * shot_count ** -0.5
    magnitude = jnp.abs(transform)
    largest = jnp.max(magnitude, axis=(0, 1))
    limits = threshold_level[0].astype(jnp.float32) * LEVEL_UNIT * (largest + 1e-6)
    factor = jnp.maximum(magnitude - limits, 0.0) / jnp.maximum(magnitude, limits)
    shrunk_real = (jnp.real(transform) * factor).astype(jnp.bfloat16)
    shrunk_imag = (jnp.imag(transform) * factor).astype(jnp.bfloat16)
    restored = jnp.fft.ifft(lax.complex(shrunk_real.astype(jnp.float32), shrunk_imag.astype(jnp.float32)), axis=0) * shot_count ** 0.5
    back_real = jnp.real(restored).astype(jnp.bfloat16)
    back_imag = jnp.imag(restored).astype(jnp.bfloat16)
    weights = jnp.where(lax.iota(jnp.int32, freq_count) == 0, 1.0, 2.0)
    weighted = lax.complex(back_real.astype(jnp.float32) * weights, back_imag.astype(jnp.float32) * weights)
    padded = jnp.pad(weighted, ((0, 0), (0, 0), (0, samples - freq_count)))
    return (jnp.real(jnp.fft.ifft(padded, axis=2)) * samples ** 0.5).astype(jnp.float32)
```

```python
import functools

import jax
import jax.numpy as jnp
import numpy as np
from jax import lax
from jax.experimental import pallas as pl
from jax.experimental.pallas import tpu as pltpu
from jax.sharding import Mesh
from jax.sharding import PartitionSpec as P

SHOTS, SAMPLES, FREQS = 1024, 1024, 512
PLACES, BLOCK = 32, 16
STEP = 24
INTERPRET = False


def time_table():
    t = np.arange(SAMPLES)[:, None]
    k = np.arange(FREQS)[None, :]
    phase = 2 * np.pi * ((t * k) % SAMPLES) / SAMPLES
    both = np.stack([np.cos(phase), -np.sin(phase)], 0).reshape(2, SAMPLES, PLACES, 16)
    return (both.transpose(1, 2, 0, 3).reshape(SAMPLES, SAMPLES) / 32).astype(jnp.bfloat16)


def time_back_table():
    t = np.arange(SAMPLES)[None, :]
    k = np.arange(FREQS)[:, None]
    phase = 2 * np.pi * ((t * k) % SAMPLES) / SAMPLES
    weight = np.where(k == 0, 1.0, 2.0) / 32
    both = np.stack([weight * np.cos(phase), -weight * np.sin(phase)], 0).reshape(2, PLACES, 16, SAMPLES)
    return both.transpose(1, 0, 2, 3).reshape(SAMPLES, SAMPLES).astype(jnp.bfloat16)


def shot_table(rows):
    q = np.arange(256)[None, :]
    phase = 2 * np.pi * ((rows[:, None] * q) % 256) / 256
    return np.concatenate([np.cos(phase), np.sin(phase)], 0).astype(jnp.bfloat16)


def twiddles(rows):
    phase = 2 * np.pi * rows[:, None] * np.arange(4)[None, :] / SHOTS
    both = np.concatenate([np.repeat(np.cos(phase), 32, 1), np.repeat(np.sin(phase), 32, 1)], 1)
    return both.astype(np.float32)


def merge_table():
    out = np.zeros((2, 2, 2, 2, 16, 2, 4, 2, 16), np.float32)
    for a1 in range(2):
        for f in range(2):
            for q1 in range(4):
                turn = np.exp(-0.5j * np.pi * (2 * f + a1) * q1)
                re, im = round(turn.real), round(turn.imag)
                for c in range(2):
                    for kk in range(16):
                        out[a1, f, c, 0, kk, 0, q1, c, kk] = re
                        out[a1, f, c, 0, kk, 1, q1, c, kk] = im
                        out[a1, f, c, 1, kk, 0, q1, c, kk] = -im
                        out[a1, f, c, 1, kk, 1, q1, c, kk] = re
    return out.reshape(256, 256).astype(jnp.bfloat16)


def split_table():
    out = np.zeros((2, 2, 4, 2, 16, 4, 2, 2, 2, 16), np.float32)
    for h in range(2):
        for q1 in range(4):
            for a in range(4):
                turn = np.exp(0.5j * np.pi * a * q1)
                re, im = round(turn.real) / 32, round(turn.imag) / 32
                for c in range(2):
                    for kk in range(16):
                        out[h, 0, q1, c, kk, a, h, c, 0, kk] = re
                        out[h, 0, q1, c, kk, a, h, c, 1, kk] = im
                        out[h, 1, q1, c, kk, a, h, c, 0, kk] = -im
                        out[h, 1, q1, c, kk, a, h, c, 1, kk] = re
    return out.reshape(512, 512).astype(jnp.bfloat16)


def back_rows():
    h, jl, i = np.meshgrid(np.arange(2), np.arange(16), np.arange(8), indexing="ij")
    return (16 * jl + 8 * h + i).reshape(-1)


def lane_ids(rows):
    return lax.broadcasted_iota(jnp.int32, (rows, 128), 1)


def rolled(value, shift):
    return value if shift % 128 == 0 else pltpu.roll(value, shift % 128, 1)


def by_group(pieces, group):
    return jnp.where(
        group < 2,
        jnp.where(group == 0, pieces[0], pieces[1]),
        jnp.where(group == 2, pieces[2], pieces[3]),
    )


def blend_kernel(lag_ref, ex_ref, low_ref, high_ref, table_hbm, out_ref, est, res, dat, upd, table, sem):
    copy = pltpu.make_async_copy(table_hbm, table, sem)
    copy.start()
    place = lax.axis_index("j")
    est[...] = jnp.zeros_like(est)
    res[...] = jnp.zeros_like(res)

    def put(ref, rows, f, row, value):
        base = (f * rows + row) * 2 * STEP + 16
        ref[pl.ds(base, 8), :] = value[:8]
        ref[pl.ds(base + STEP, 8), :] = value[8:]

    at_start = jnp.where(place == 0, 1, 0)
    at_end = jnp.where(place == PLACES - 1, 1, 0)
    for f in range(2):
        low = jnp.where(at_start == 1, 1 - f, f)
        high = jnp.where(at_end == 1, 1 - f, f)
        for i in range(2):
            put(est, 20, f, i, low_ref[low, i].astype(jnp.float32))
            put(est, 20, f, 18 + i, high_ref[high, i].astype(jnp.float32))
        dat[f * 18] = low_ref[low, 2].astype(jnp.float32)
        dat[f * 18 + 17] = high_ref[high, 2].astype(jnp.float32)
        for i in range(BLOCK):
            put(est, 20, f, i + 2, ex_ref[f, i, 0].astype(jnp.float32))
            dat[f * 18 + i + 1] = ex_ref[f, i, 1].astype(jnp.float32)

    lanes = lane_ids(8)

    def companions(ref, rows, f, row, shot):
        fleet = ((shot + 1) >> 9) & 1
        own = shot * 6 + 3 * fleet
        other = shot * 6 + 3 - 3 * fleet
        total = [None, None]
        for at, side, step in ((own, 0, -1), (own + 2, 0, 1), (other, 1, -1), (other + 1, 1, 0), (other + 2, 1, 1)):
            lag = lag_ref[at]
            turn = lag & 127
            keep = lanes < 128 - turn
            first = ((f ^ side) * rows + row + step) * 2 * STEP + 16 - (lag >> 7)
            for c in range(2):
                here = ref[pl.ds(first + c * STEP, 8), :]
                before = ref[pl.ds(first + c * STEP - 1, 8), :]
                moved = pltpu.roll(jnp.where(keep, here, before), turn, 1)
                total[c] = moved if total[c] is None else total[c] + moved
        return total

    def rows_of(ref, rows, f, row):
        base = (f * rows + row) * 2 * STEP + 16
        return ref[pl.ds(base, 8), :], ref[pl.ds(base + STEP, 8), :]

    @pl.loop(0, 18)
    def _(n):
        for f in range(2):
            shot = (512 * f + BLOCK * place + n - 1 + SHOTS) & (SHOTS - 1)
            total = companions(est, 20, f, n + 1, shot)
            own = rows_of(est, 20, f, n + 1)
            data = dat[f * 18 + n]
            base = (f * 18 + n) * 2 * STEP + 16
            for c in range(2):
                value = data[8 * c : 8 * c + 8] - own[c] - total[c]
                ref_value = value.astype(jnp.bfloat16).astype(jnp.float32)
                res[pl.ds(base + c * STEP, 8), :] = ref_value

    @pl.loop(0, BLOCK)
    def _(n):
        for f in range(2):
            shot = (512 * f + BLOCK * place + n) & (SHOTS - 1)
            total = companions(res, 18, f, n + 1, shot)
            own = rows_of(est, 20, f, n + 2)
            left = rows_of(res, 18, f, n + 1)
            for c in range(2):
                value = own[c] + 0.25 * (left[c] + total[c])
                upd[pl.ds(((f * 2 + c) * BLOCK + n) * 8, 8), :] = value

    parts = [upd[pl.ds(u, 64, stride=8), :] for u in range(8)]
    lhs = jnp.concatenate(parts, 1).astype(jnp.bfloat16)
    copy.wait()
    group = lane_ids(BLOCK) // 32
    for half in range(4):
        product = jnp.dot(lhs, table[:, 256 * half : 256 * half + 256], preferred_element_type=jnp.float32)
        for m in range(2):
            block = product[:, 128 * m : 128 * m + 128]
            turned = [[rolled(block[16 * g : 16 * g + 16], 32 * k) for k in range(4)] for g in range(4)]
            for d in range(4):
                chunk = by_group([turned[g][(g - d) % 4] for g in range(4)], group)
                out_ref[8 * half + 4 * m + d] = chunk.astype(jnp.bfloat16)


def forward_kernel(x_ref, merge_ref, turn_ref, shots_ref, spec_ref, peak_ref):
    lhs = jnp.concatenate([x_ref[:256], x_ref[256:]], 1)
    merged = jnp.dot(lhs, merge_ref[...], preferred_element_type=jnp.float32)
    re, im = merged[:, :128], merged[:, 128:]
    cos, sin = turn_ref[:, :128], turn_ref[:, 128:]
    rhs = jnp.concatenate([re * cos + im * sin, im * cos - re * sin], 1).astype(jnp.bfloat16)
    product = jnp.dot(shots_ref[...], rhs, preferred_element_type=jnp.float32) * (1 / 32)
    re = product[:256, :128] + product[256:, 128:]
    im = product[:256, 128:] - product[256:, :128]
    spec_ref[:, :128] = re
    spec_ref[:, 128:] = im
    peak = jnp.max(re * re + im * im, axis=0, keepdims=True)
    peak = jnp.broadcast_to(peak, (8, 128))
    for shift in (16, 32, 64):
        peak = jnp.maximum(peak, pltpu.roll(peak, shift, 1))
    peak_ref[...] = jnp.broadcast_to(peak[None], peak_ref.shape)


def backward_kernel(level_ref, spec_ref, peak_ref, shots_ref, turn_ref, split_ref, out_ref):
    peak = jnp.sqrt(jnp.max(peak_ref[...].reshape(-1, 128), axis=0, keepdims=True))
    limit = level_ref[0].astype(jnp.float32) * (1 / 64) * (peak + 1e-6)
    re, im = spec_ref[:, :128], spec_ref[:, 128:]
    size = jnp.sqrt(re * re + im * im)
    factor = jnp.maximum(size - limit, 0.0) / jnp.maximum(size, limit)
    rhs = jnp.concatenate([re * factor, im * factor], 1).astype(jnp.bfloat16)
    product = jnp.dot(shots_ref[...], rhs, preferred_element_type=jnp.float32)
    re = product[:256, :128] - product[256:, 128:]
    im = product[:256, 128:] + product[256:, :128]
    cos, sin = turn_ref[:, :128], turn_ref[:, 128:]
    turned = jnp.concatenate([re * cos - im * sin, im * cos + re * sin], 1).astype(jnp.bfloat16)
    lhs = jnp.concatenate([turned[:128], turned[128:]], 1)
    product = jnp.dot(lhs, split_ref[...], preferred_element_type=jnp.float32)
    for a in range(4):
        out_ref[128 * a : 128 * a + 128] = product[:, 128 * a : 128 * a + 128].astype(jnp.bfloat16)


def time_back_kernel(x_ref, table_ref, out_ref, lhs):
    x = x_ref[...].astype(jnp.float32)
    group = lane_ids(8) // 32
    for zh in range(2):
        for m in range(8):
            tiles = [x[(zh * 32 + 4 * m + d) * 8 :][:8] for d in range(4)]
            turned = [[rolled(tiles[d], 32 * k) for k in range(4)] for d in range(4)]
            for g in range(4):
                piece = by_group([turned[d][(d - g) % 4] for d in range(4)], group)
                lhs[(zh * 4 + g) * 8 : (zh * 4 + g) * 8 + 8, 128 * m : 128 * m + 128] = piece
    left = lhs[...].astype(jnp.bfloat16)
    for n in range(4):
        columns = slice(256 * n, 256 * n + 256)
        product = jnp.dot(left, table_ref[:, columns], preferred_element_type=jnp.float32)
        for zh in range(2):
            for h in range(2):
                for c in range(2):
                    row = (zh * 4 + 2 * h + c) * 8
                    out_ref[8 * h : 8 * h + 8, 2 * zh + c, columns] = product[row : row + 8]


def vmem(count):
    return [pl.BlockSpec(memory_space=pltpu.VMEM)] * count


def smem():
    return pl.BlockSpec(memory_space=pltpu.SMEM)


PARAMS = pltpu.CompilerParams(vmem_limit_bytes=32 * 1024 * 1024)


def call(kernel, outs, in_specs, scratch=(), out_count=1):
    return pl.pallas_call(
        kernel,
        out_shape=outs,
        in_specs=in_specs,
        out_specs=vmem(out_count) if out_count > 1 else vmem(1)[0],
        scratch_shapes=list(scratch),
        compiler_params=PARAMS,
        interpret=INTERPRET,
    )


def local(blended, estimate, neighbour_sources, partner_lags, threshold_level):
    lags = lax.all_gather(partner_lags.reshape(-1), ("zh", "j"), axis=0, tiled=True)
    both = jnp.stack([estimate, blended.astype(jnp.bfloat16)], 1)
    both = both.reshape(BLOCK, 2, 2, 16, 128).transpose(2, 0, 1, 3, 4)
    ex = lax.all_to_all(both, "zh", 0, 0, tiled=True)
    up = jnp.concatenate([ex[:, 14:, 0], ex[:, 15:, 1]], 1)
    down = jnp.concatenate([ex[:, :2, 0], ex[:, :1, 1]], 1)
    low = lax.ppermute(up, "j", [(i, (i + 1) % PLACES) for i in range(PLACES)])
    high = lax.ppermute(down, "j", [((i + 1) % PLACES, i) for i in range(PLACES)])
    send = call(
        blend_kernel,
        jax.ShapeDtypeStruct((PLACES, BLOCK, 128), jnp.bfloat16),
        [smem()] + vmem(3) + [pl.BlockSpec(memory_space=pl.ANY)],
        [
            pltpu.VMEM((80 * STEP + 16, 128), jnp.float32),
            pltpu.VMEM((72 * STEP + 16, 128), jnp.float32),
            pltpu.VMEM((36, 16, 128), jnp.float32),
            pltpu.VMEM((512, 128), jnp.float32),
            pltpu.VMEM((SAMPLES, SAMPLES), jnp.bfloat16),
            pltpu.SemaphoreType.DMA,
        ],
    )(lags, ex, low, high, time_table())
    columns = lax.all_to_all(send, "j", 0, 0, tiled=True).reshape(512, 128)
    others = lax.axis_size("zh") * lax.axis_size("chan")
    spec, peak = call(
        forward_kernel,
        (jax.ShapeDtypeStruct((256, 256), jnp.float32), jax.ShapeDtypeStruct((others, 8, 128), jnp.float32)),
        vmem(4),
        out_count=2,
    )(columns, merge_table(), twiddles(np.arange(256)), shot_table(np.arange(256)))
    peaks = lax.all_to_all(peak, ("zh", "chan"), 0, 0, tiled=True)
    rows = back_rows()
    back = call(
        backward_kernel,
        jax.ShapeDtypeStruct((512, 128), jnp.bfloat16),
        [smem()] + vmem(5),
    )(threshold_level, spec, peaks, shot_table(rows), twiddles(rows), split_table())
    arrived = lax.all_to_all(back.reshape(64, 8, 128), ("zh", "j"), 0, 0, tiled=True).reshape(512, 128)
    return call(
        time_back_kernel,
        jax.ShapeDtypeStruct((BLOCK, 4, SAMPLES), jnp.float32),
        vmem(2),
        [pltpu.VMEM((64, SAMPLES), jnp.float32)],
    )(arrived, time_back_table())


def solution(mesh):
    split = Mesh(mesh.devices.reshape(2, PLACES, -1), ("zh", "j", "chan"))
    shots = P(("zh", "j"), "chan", None)
    return jax.shard_map(
        local,
        mesh=split,
        in_specs=(shots, shots, P(("zh", "j"), None), P(("zh", "j"), None), P()),
        out_specs=shots,
        check_vma=False,
    )
```

```python
import functools

import jax
import jax.numpy as jnp
import numpy as np
from jax import lax
from jax.experimental import pallas as pl
from jax.experimental.pallas import tpu as pltpu
from jax.sharding import Mesh
from jax.sharding import PartitionSpec as P

SHOTS, SAMPLES, FREQS = 1024, 1024, 512
PLACES, BLOCK = 32, 16
STEP = 24
INTERPRET = False


def time_table():
    t = np.arange(SAMPLES)[:, None]
    k = np.arange(FREQS)[None, :]
    phase = 2 * np.pi * ((t * k) % SAMPLES) / SAMPLES
    both = np.stack([np.cos(phase), -np.sin(phase)], 0).reshape(2, SAMPLES, PLACES, 16)
    return (both.transpose(1, 2, 0, 3).reshape(SAMPLES, SAMPLES) / 32).astype(jnp.bfloat16)


def time_back_table():
    t = np.arange(SAMPLES)[None, :]
    k = np.arange(FREQS)[:, None]
    phase = 2 * np.pi * ((t * k) % SAMPLES) / SAMPLES
    weight = np.where(k == 0, 1.0, 2.0) / 32
    both = np.stack([weight * np.cos(phase), -weight * np.sin(phase)], 0).reshape(2, PLACES, 16, SAMPLES)
    return both.transpose(1, 0, 2, 3).reshape(SAMPLES, SAMPLES).astype(jnp.bfloat16)


def shot_table(rows):
    q = np.arange(256)[None, :]
    phase = 2 * np.pi * ((rows[:, None] * q) % 256) / 256
    return np.concatenate([np.cos(phase), np.sin(phase)], 0).astype(jnp.bfloat16)


def twiddles(rows):
    phase = 2 * np.pi * rows[:, None] * np.arange(4)[None, :] / SHOTS
    both = np.concatenate([np.repeat(np.cos(phase), 32, 1), np.repeat(np.sin(phase), 32, 1)], 1)
    return both.astype(np.float32)


def merge_table():
    out = np.zeros((2, 2, 2, 2, 16, 2, 4, 2, 16), np.float32)
    for a1 in range(2):
        for f in range(2):
            for q1 in range(4):
                turn = np.exp(-0.5j * np.pi * (2 * f + a1) * q1)
                re, im = round(turn.real), round(turn.imag)
                for c in range(2):
                    for kk in range(16):
                        out[a1, f, c, 0, kk, 0, q1, c, kk] = re
                        out[a1, f, c, 0, kk, 1, q1, c, kk] = im
                        out[a1, f, c, 1, kk, 0, q1, c, kk] = -im
                        out[a1, f, c, 1, kk, 1, q1, c, kk] = re
    return out.reshape(256, 256).astype(jnp.bfloat16)


def split_table():
    out = np.zeros((2, 2, 4, 2, 16, 4, 2, 2, 2, 16), np.float32)
    for h in range(2):
        for q1 in range(4):
            for a in range(4):
                turn = np.exp(0.5j * np.pi * a * q1)
                re, im = round(turn.real) / 32, round(turn.imag) / 32
                for c in range(2):
                    for kk in range(16):
                        out[h, 0, q1, c, kk, a, h, c, 0, kk] = re
                        out[h, 0, q1, c, kk, a, h, c, 1, kk] = im
                        out[h, 1, q1, c, kk, a, h, c, 0, kk] = -im
                        out[h, 1, q1, c, kk, a, h, c, 1, kk] = re
    return out.reshape(512, 512).astype(jnp.bfloat16)


def back_rows():
    h, jl, i = np.meshgrid(np.arange(2), np.arange(16), np.arange(8), indexing="ij")
    return (16 * jl + 8 * h + i).reshape(-1)


def lane_ids(rows):
    return lax.broadcasted_iota(jnp.int32, (rows, 128), 1)


def rolled(value, shift):
    return value if shift % 128 == 0 else pltpu.roll(value, shift % 128, 1)


def by_group(pieces, group):
    return jnp.where(
        group < 2,
        jnp.where(group == 0, pieces[0], pieces[1]),
        jnp.where(group == 2, pieces[2], pieces[3]),
    )


def blend_kernel(
    ex_ref, low_ref, high_ref, table_hbm, out_ref, est, res, dat, upd, table, lag_vmem, lag_ref, sem, lag_sem
):
    copy = pltpu.make_async_copy(table_hbm, table, sem)
    copy.start()
    place = lax.axis_index("j")
    est[...] = jnp.zeros_like(est)
    res[...] = jnp.zeros_like(res)

    def put(ref, rows, f, row, value):
        base = (f * rows + row) * 2 * STEP + 16
        ref[pl.ds(base, 8), :] = value[:8]
        ref[pl.ds(base + STEP, 8), :] = value[8:]

    at_start = jnp.where(place == 0, 1, 0)
    at_end = jnp.where(place == PLACES - 1, 1, 0)
    for f in range(2):
        low = jnp.where(at_start == 1, 1 - f, f)
        high = jnp.where(at_end == 1, 1 - f, f)
        coded = jnp.concatenate([r.astype(jnp.float32) for r in (low_ref[low, 3], ex_ref[f, 32], high_ref[high, 3])], 0)
        lag_vmem[f] = (32.0 * coded + pltpu.roll(coded, 120, 1)).astype(jnp.int32)
    lag_copy = pltpu.make_async_copy(lag_vmem, lag_ref, lag_sem)
    lag_copy.start()
    for f in range(2):
        low = jnp.where(at_start == 1, 1 - f, f)
        high = jnp.where(at_end == 1, 1 - f, f)
        for i in range(2):
            put(est, 20, f, i, low_ref[low, i].astype(jnp.float32))
            put(est, 20, f, 18 + i, high_ref[high, i].astype(jnp.float32))
        dat[f * 18] = low_ref[low, 2].astype(jnp.float32)
        dat[f * 18 + 17] = high_ref[high, 2].astype(jnp.float32)
        for i in range(BLOCK):
            put(est, 20, f, i + 2, ex_ref[f, i].astype(jnp.float32))
            dat[f * 18 + i + 1] = ex_ref[f, BLOCK + i].astype(jnp.float32)

    lag_copy.wait()
    lanes = lane_ids(8)

    def companions(ref, rows, f, row, n):
        fleet = ((512 * f + BLOCK * place + n + SHOTS + 1) >> 9) & 1
        own = 3 * fleet
        other = 3 - 3 * fleet
        total = [None, None]
        for at, side, step in ((own, 0, -1), (own + 2, 0, 1), (other, 1, -1), (other + 1, 1, 0), (other + 2, 1, 1)):
            lag = lag_ref[f, BLOCK + n, at]
            turn = lag & 127
            keep = lanes < 128 - turn
            first = ((f ^ side) * rows + row + step) * 2 * STEP + 16 - (lag >> 7)
            for c in range(2):
                here = ref[pl.ds(first + c * STEP, 8), :]
                before = ref[pl.ds(first + c * STEP - 1, 8), :]
                moved = pltpu.roll(jnp.where(keep, here, before), turn, 1)
                total[c] = moved if total[c] is None else total[c] + moved
        return total

    def rows_of(ref, rows, f, row):
        base = (f * rows + row) * 2 * STEP + 16
        return ref[pl.ds(base, 8), :], ref[pl.ds(base + STEP, 8), :]

    @pl.loop(0, 18)
    def _(n):
        for f in range(2):
            total = companions(est, 20, f, n + 1, n - 1)
            own = rows_of(est, 20, f, n + 1)
            data = dat[f * 18 + n]
            base = (f * 18 + n) * 2 * STEP + 16
            for c in range(2):
                value = data[8 * c : 8 * c + 8] - own[c] - total[c]
                ref_value = value.astype(jnp.bfloat16).astype(jnp.float32)
                res[pl.ds(base + c * STEP, 8), :] = ref_value

    @pl.loop(0, BLOCK)
    def _(n):
        for f in range(2):
            total = companions(res, 18, f, n + 1, n)
            own = rows_of(est, 20, f, n + 2)
            left = rows_of(res, 18, f, n + 1)
            for c in range(2):
                value = own[c] + 0.25 * (left[c] + total[c])
                upd[pl.ds(((f * 2 + c) * BLOCK + n) * 8, 8), :] = value

    parts = [upd[pl.ds(u, 64, stride=8), :] for u in range(8)]
    lhs = jnp.concatenate(parts, 1).astype(jnp.bfloat16)
    copy.wait()
    group = lane_ids(BLOCK) // 32
    for half in range(4):
        product = jnp.dot(lhs, table[:, 256 * half : 256 * half + 256], preferred_element_type=jnp.float32)
        for m in range(2):
            block = product[:, 128 * m : 128 * m + 128]
            turned = [[rolled(block[16 * g : 16 * g + 16], 32 * k) for k in range(4)] for g in range(4)]
            for d in range(4):
                chunk = by_group([turned[g][(g - d) % 4] for g in range(4)], group)
                out_ref[8 * half + 4 * m + d] = chunk.astype(jnp.bfloat16)


def forward_kernel(x_ref, merge_ref, turn_ref, shots_ref, spec_ref, peak_ref):
    lhs = jnp.concatenate([x_ref[:256], x_ref[256:]], 1)
    merged = jnp.dot(lhs, merge_ref[...], preferred_element_type=jnp.float32)
    re, im = merged[:, :128], merged[:, 128:]
    cos, sin = turn_ref[:, :128], turn_ref[:, 128:]
    rhs = jnp.concatenate([re * cos + im * sin, im * cos - re * sin], 1).astype(jnp.bfloat16)
    product = jnp.dot(shots_ref[...], rhs, preferred_element_type=jnp.float32) * (1 / 32)
    re = product[:256, :128] + product[256:, 128:]
    im = product[:256, 128:] - product[256:, :128]
    spec_ref[:, :128] = re
    spec_ref[:, 128:] = im
    peak = jnp.max(re * re + im * im, axis=0, keepdims=True)
    peak = jnp.broadcast_to(peak, (8, 128))
    for shift in (16, 32, 64):
        peak = jnp.maximum(peak, pltpu.roll(peak, shift, 1))
    peak_ref[...] = jnp.broadcast_to(peak[None], peak_ref.shape)


def backward_kernel(level_ref, spec_ref, peak_ref, shots_ref, turn_ref, split_ref, out_ref):
    peak = jnp.sqrt(jnp.max(peak_ref[...].reshape(-1, 128), axis=0, keepdims=True))
    limit = level_ref[0].astype(jnp.float32) * (1 / 64) * (peak + 1e-6)
    re, im = spec_ref[:, :128], spec_ref[:, 128:]
    size = jnp.sqrt(re * re + im * im)
    factor = jnp.maximum(size - limit, 0.0) / jnp.maximum(size, limit)
    rhs = jnp.concatenate([re * factor, im * factor], 1).astype(jnp.bfloat16)
    product = jnp.dot(shots_ref[...], rhs, preferred_element_type=jnp.float32)
    re = product[:256, :128] - product[256:, 128:]
    im = product[:256, 128:] + product[256:, :128]
    cos, sin = turn_ref[:, :128], turn_ref[:, 128:]
    turned = jnp.concatenate([re * cos - im * sin, im * cos + re * sin], 1).astype(jnp.bfloat16)
    lhs = jnp.concatenate([turned[:128], turned[128:]], 1)
    product = jnp.dot(lhs, split_ref[...], preferred_element_type=jnp.float32)
    for a in range(4):
        out_ref[128 * a : 128 * a + 128] = product[:, 128 * a : 128 * a + 128].astype(jnp.bfloat16)


def time_back_kernel(x_ref, table_ref, out_ref, lhs):
    x = x_ref[...].astype(jnp.float32)
    group = lane_ids(8) // 32
    for zh in range(2):
        for m in range(8):
            tiles = [x[(zh * 32 + 4 * m + d) * 8 :][:8] for d in range(4)]
            turned = [[rolled(tiles[d], 32 * k) for k in range(4)] for d in range(4)]
            for g in range(4):
                piece = by_group([turned[d][(d - g) % 4] for d in range(4)], group)
                lhs[(zh * 4 + g) * 8 : (zh * 4 + g) * 8 + 8, 128 * m : 128 * m + 128] = piece
    left = lhs[...].astype(jnp.bfloat16)
    for n in range(4):
        columns = slice(256 * n, 256 * n + 256)
        product = jnp.dot(left, table_ref[:, columns], preferred_element_type=jnp.float32)
        for zh in range(2):
            for h in range(2):
                for c in range(2):
                    row = (zh * 4 + 2 * h + c) * 8
                    out_ref[8 * h : 8 * h + 8, 2 * zh + c, columns] = product[row : row + 8]


def vmem(count):
    return [pl.BlockSpec(memory_space=pltpu.VMEM)] * count


def smem():
    return pl.BlockSpec(memory_space=pltpu.SMEM)


PARAMS = pltpu.CompilerParams(vmem_limit_bytes=32 * 1024 * 1024)


def call(kernel, outs, in_specs, scratch=(), out_count=1):
    return pl.pallas_call(
        kernel,
        out_shape=outs,
        in_specs=in_specs,
        out_specs=vmem(out_count) if out_count > 1 else vmem(1)[0],
        scratch_shapes=list(scratch),
        compiler_params=PARAMS,
        interpret=INTERPRET,
    )


def local(blended, estimate, neighbour_sources, partner_lags, threshold_level):
    est = estimate.reshape(BLOCK, 2, 16, 128)
    data = blended.astype(jnp.bfloat16).reshape(BLOCK, 2, 16, 128)
    lags = jnp.pad(jnp.concatenate([jnp.pad(partner_lags >> 5, ((0, 0), (0, 2))), partner_lags & 31], 1), ((0, 0), (0, 114)))
    lags = jnp.broadcast_to(lags.astype(jnp.bfloat16)[None, None], (1, 2, 16, 128))
    both = jnp.concatenate([est, data, lags], 0).transpose(1, 0, 2, 3)
    ex = lax.all_to_all(both, "zh", 0, 0, tiled=True)
    up = jnp.concatenate([ex[:, 14:16], ex[:, 31:33]], 1)
    down = jnp.concatenate([ex[:, :2], ex[:, 16:17], ex[:, 32:]], 1)
    low = lax.ppermute(up, "j", [(i, (i + 1) % PLACES) for i in range(PLACES)])
    high = lax.ppermute(down, "j", [((i + 1) % PLACES, i) for i in range(PLACES)])
    send = call(
        blend_kernel,
        jax.ShapeDtypeStruct((PLACES, BLOCK, 128), jnp.bfloat16),
        vmem(3) + [pl.BlockSpec(memory_space=pl.ANY)],
        [
            pltpu.VMEM((80 * STEP + 16, 128), jnp.float32),
            pltpu.VMEM((72 * STEP + 16, 128), jnp.float32),
            pltpu.VMEM((36, 16, 128), jnp.float32),
            pltpu.VMEM((512, 128), jnp.float32),
            pltpu.VMEM((SAMPLES, SAMPLES), jnp.bfloat16),
            pltpu.VMEM((2, 48, 128), jnp.int32),
            pltpu.SMEM((2, 48, 128), jnp.int32),
            pltpu.SemaphoreType.DMA,
            pltpu.SemaphoreType.DMA,
        ],
    )(ex, low, high, time_table())
    columns = lax.all_to_all(send, "j", 0, 0, tiled=True).reshape(512, 128)
    others = lax.axis_size("zh") * lax.axis_size("chan")
    spec, peak = call(
        forward_kernel,
        (jax.ShapeDtypeStruct((256, 256), jnp.float32), jax.ShapeDtypeStruct((others, 8, 128), jnp.float32)),
        vmem(4),
        out_count=2,
    )(columns, merge_table(), twiddles(np.arange(256)), shot_table(np.arange(256)))
    peaks = lax.all_to_all(peak, ("zh", "chan"), 0, 0, tiled=True)
    rows = back_rows()
    back = call(
        backward_kernel,
        jax.ShapeDtypeStruct((512, 128), jnp.bfloat16),
        [smem()] + vmem(5),
    )(threshold_level, spec, peaks, shot_table(rows), twiddles(rows), split_table())
    arrived = lax.all_to_all(back.reshape(64, 8, 128), ("zh", "j"), 0, 0, tiled=True).reshape(512, 128)
    return call(
        time_back_kernel,
        jax.ShapeDtypeStruct((BLOCK, 4, SAMPLES), jnp.float32),
        vmem(2),
        [pltpu.VMEM((64, SAMPLES), jnp.float32)],
    )(arrived, time_back_table())


def solution(mesh):
    split = Mesh(mesh.devices.reshape(2, PLACES, -1), ("zh", "j", "chan"))
    shots = P(("zh", "j"), "chan", None)
    return jax.shard_map(
        local,
        mesh=split,
        in_specs=(shots, shots, P(("zh", "j"), None), P(("zh", "j"), None), P()),
        out_specs=shots,
        check_vma=False,
    )
```

```python
import jax
import jax.numpy as jnp
import numpy as np
from jax import lax
from jax.experimental import pallas as pl
from jax.experimental.pallas import tpu as pltpu
from jax.sharding import PartitionSpec as P

SHOTS, SAMPLES, FREQS = 1024, 1024, 512
DEVS, BLOCK, CHANS = 64, 16, 4
STEP = 24
INTERPRET = False


def time_table():
    t = np.arange(SAMPLES)[None, :]
    k = np.arange(FREQS)[:, None]
    phase = 2 * np.pi * ((t * k) % SAMPLES) / SAMPLES
    return (np.concatenate([np.cos(phase), -np.sin(phase)], 0) / 32).astype(jnp.bfloat16)


def time_back_table():
    t = np.arange(SAMPLES)[None, :]
    k = np.arange(FREQS)[:, None]
    phase = 2 * np.pi * ((t * k) % SAMPLES) / SAMPLES
    weight = np.where(k == 0, 1.0, 2.0) / 32
    return np.concatenate([weight * np.cos(phase), -weight * np.sin(phase)], 0).astype(jnp.bfloat16)


def place_table():
    phase = 2 * np.pi * (np.arange(64)[:, None] * np.arange(64)[None, :] % 64) / 64
    return np.concatenate([np.cos(phase), np.sin(phase)], 0).astype(jnp.bfloat16)


def twiddles():
    phase = 2 * np.pi * np.arange(64)[:, None] * np.arange(BLOCK)[None, :] / SHOTS
    cos, sin = np.tile(np.cos(phase), (1, 8)), np.tile(np.sin(phase), (1, 8))
    sin[:, 64:] *= -1
    return np.concatenate([cos, sin], 1).astype(np.float32)


def block_table(sign):
    out = np.zeros((2, CHANS, 16, 2, CHANS, 16), np.float64)
    phase = 2 * np.pi * (np.arange(16)[:, None] * np.arange(16)[None, :] % 16) / 16
    for c in range(CHANS):
        out[0, c, :, 0, c, :] = np.cos(phase)
        out[1, c, :, 1, c, :] = np.cos(phase)
        out[0, c, :, 1, c, :] = sign * np.sin(phase)
        out[1, c, :, 0, c, :] = -sign * np.sin(phase)
    return (out.reshape(128, 128) / 32).astype(jnp.bfloat16)


def lane_ids(*shape):
    return lax.broadcasted_iota(jnp.int32, (*shape, 128), len(shape))


def swapped(value):
    return pltpu.roll(value, 64, value.ndim - 1)


def blend_kernel(lag_ref, dat_ref, est_ref, table_hbm, out_ref, tmp, est, res, upd, acc, table, sem):
    copy = pltpu.make_async_copy(table_hbm, table, sem)
    copy.start()
    place = lax.axis_index("shot")
    est[...] = jnp.zeros_like(est)
    res[...] = jnp.zeros_like(res)
    upd[1024:, :] = jnp.zeros((1024, 128), jnp.float32)
    tmp[...] = est_ref[...].astype(jnp.float32)

    def base(row, c):
        return (row * CHANS + c) * STEP + 16

    for c in range(CHANS):
        for u in range(8):
            columns = slice(128 * u, 128 * u + 128)
            old = tmp[:, c, columns]
            est[pl.ds(base(2, c) + u, BLOCK, stride=CHANS * STEP), :] = old
            res[pl.ds(base(3, c) + u, BLOCK, stride=CHANS * STEP), :] = dat_ref[:, c, columns] - old

    lanes = lane_ids(8)

    def companions(ref, row_of, side, n, kinds):
        shot = (512 * side + BLOCK * place + n + SHOTS) & (SHOTS - 1)
        fleet = ((shot + 1) >> 9) & 1
        own = (shot & 15) * 6 + 3 * fleet
        other = (shot & 15) * 6 + 3 - 3 * fleet
        slots = ((own, 0, -1), (own + 2, 0, 1), (other, 1, -1), (other + 1, 1, 0), (other + 2, 1, 1))
        total = [None] * CHANS
        for at, flip, step in slots:
            if flip not in kinds:
                continue
            lag = lag_ref[shot >> 4, at]
            turn = lag & 127
            keep = lanes < 128 - turn
            first = base(row_of(side ^ flip, n + step), 0) - (lag >> 7)
            for c in range(CHANS):
                here = ref[pl.ds(first + c * STEP, 8), :]
                before = ref[pl.ds(first + c * STEP - 1, 8), :]
                moved = pltpu.roll(jnp.where(keep, here, before), turn, 1)
                total[c] = moved if total[c] is None else total[c] + moved
        return total

    def est_row(side, n):
        return n + 2

    def res_row(side, n):
        return side * 22 + n + 3

    @pl.loop(0, BLOCK + 2)
    def _(step):
        n = step - 1
        near = companions(est, est_row, 0, n, (0,))
        far = companions(est, est_row, 1, n, (1,))
        for c in range(CHANS):
            rows = pl.ds(base(res_row(0, n), c), 8)
            res[rows, :] = res[rows, :] - near[c]
            res[pl.ds(base(res_row(1, n), c), 8), :] = -far[c]

    @pl.loop(0, BLOCK + 4)
    def _(step):
        n = step - 2
        for side in range(2):
            total = companions(res, res_row, side, n, (0, 1))
            low = 128 + (14 if side == 0 else 12) + n + 2
            high = 128 + (0 if side == 0 else 2) + n - 16
            at = jnp.where(n < 0, low, jnp.where(n > 15, high, side * 64 + n))
            for c in range(CHANS):
                value = 0.25 * (total[c] + res[pl.ds(base(res_row(side, n), c), 8), :])
                if side == 0:
                    value = value + est[pl.ds(base(n + 2, c), 8), :]
                upd[pl.ds((at + c * BLOCK) * 8, 8), :] = value

    rows = jnp.concatenate([upd[pl.ds(u, 256, stride=8), :] for u in range(8)], 1).astype(jnp.bfloat16)
    copy.wait()
    rims = None
    for ri in range(2):
        product = lax.dot_general(
            table[512 * ri : 512 * ri + 512, :],
            rows,
            (((1,), (1,)), ((), ())),
            preferred_element_type=jnp.float32,
        )
        acc[:, 8 * ri : 8 * ri + 8, :] = product[:, :128].reshape(DEVS, 8, 128)
        rims = product[:, 128:] if rims is None else rims + swapped(product[:, 128:])
    acc[:, 16:24, :] = rims.reshape(DEVS, 8, 128)
    out_ref[...] = acc[...].reshape(DEVS * 24, 128).astype(jnp.bfloat16)


def forward_kernel(x_ref, place_ref, turn_ref, block_ref, spec_ref, peak_ref, tmp):
    x = x_ref[...].astype(jnp.float32).reshape(DEVS, 24, 128)
    real, imag, rims = x[:, :8], x[:, 8:16], x[:, 16:]

    def ahead(value, count):
        return jnp.concatenate([value[count:], value[:count]], 0)

    def lane_roll(value, shift):
        return pltpu.roll(value.reshape(512, 128), shift, 1).reshape(DEVS, 8, 128)

    lanes = lane_ids(DEVS, 8)
    within = lanes & 15
    total = jnp.where(
        lanes < 64,
        real + lane_roll(ahead(real, 32), 64),
        lane_roll(imag, 64) + ahead(imag, 32),
    )
    far = ahead(rims, 32)
    rims = rims + jnp.where(within < 8, lane_roll(far, 126), lane_roll(far, 2))
    total = total + jnp.where(within < 2, ahead(rims, 63), jnp.where(within >= 14, ahead(rims, 1), 0.0))
    tmp[...] = total.reshape(512, 128)
    rhs = jnp.concatenate([tmp[pl.ds(kk, 64, stride=8), :] for kk in range(8)], 1).astype(jnp.bfloat16)
    product = jnp.dot(place_ref[...], rhs, preferred_element_type=jnp.float32)
    cos, sin = turn_ref[:, :128], turn_ref[:, 128:]
    half = lane_ids(64) < 64
    turned = []
    for kk in range(8):
        columns = slice(128 * kk, 128 * kk + 128)
        other = swapped(product[64:, columns])
        value = product[:64, columns] + jnp.where(half, other, -other)
        turned.append((value * cos + swapped(value) * sin).astype(jnp.bfloat16))
    spec = jnp.dot(jnp.concatenate(turned, 0), block_ref[...], preferred_element_type=jnp.float32)
    spec_ref[...] = spec
    square = spec * spec
    square = square + swapped(square)
    peak = jnp.concatenate(
        [jnp.max(square[64 * kk : 64 * kk + 64], axis=0, keepdims=True) for kk in range(8)], 0
    )
    for shift in (1, 2, 4, 8, 16, 32):
        peak = jnp.maximum(peak, pltpu.roll(peak, shift, 1))
    peak_ref[...] = jnp.broadcast_to(peak[None], peak_ref.shape)


def backward_kernel(level_ref, spec_ref, peak_ref, place_ref, turn_ref, block_ref, out_ref, tmp):
    peak = jnp.sqrt(jnp.max(peak_ref[...], axis=0))
    limit = level_ref[0].astype(jnp.float32) * (1 / 64) * (peak + 1e-6)
    shrunk = []
    for kk in range(8):
        value = spec_ref[64 * kk : 64 * kk + 64, :]
        square = value * value
        size = jnp.sqrt(square + swapped(square))
        bound = limit[kk : kk + 1]
        factor = jnp.maximum(size - bound, 0.0) / jnp.maximum(size, bound)
        shrunk.append((value * factor).astype(jnp.bfloat16))
    product = jnp.dot(jnp.concatenate(shrunk, 0), block_ref[...], preferred_element_type=jnp.float32)
    cos, sin = turn_ref[:, :128], turn_ref[:, 128:]
    turned = []
    for kk in range(8):
        value = product[64 * kk : 64 * kk + 64]
        turned.append((value * cos - swapped(value) * sin).astype(jnp.bfloat16))
    product = jnp.dot(place_ref[...], jnp.concatenate(turned, 1), preferred_element_type=jnp.float32)
    half = lane_ids(64) < 64
    for kk in range(8):
        columns = slice(128 * kk, 128 * kk + 128)
        other = swapped(product[64:, columns])
        tmp[pl.ds(kk, 64, stride=8), :] = product[:64, columns] - jnp.where(half, other, -other)
    out_ref[...] = tmp[...].astype(jnp.bfloat16)


def time_back_kernel(x_ref, table_ref, out_ref):
    turned = x_ref[...].astype(jnp.float32).T.astype(jnp.bfloat16)
    left = jnp.concatenate([turned[:64], turned[64:]], 1)
    for n in range(4):
        columns = slice(256 * n, 256 * n + 256)
        product = jnp.dot(left, table_ref[:, columns], preferred_element_type=jnp.float32)
        for c in range(CHANS):
            out_ref[:, c, columns] = product[BLOCK * c : BLOCK * c + BLOCK]


def vmem(count):
    return [pl.BlockSpec(memory_space=pltpu.VMEM)] * count


def smem():
    return pl.BlockSpec(memory_space=pltpu.SMEM)


def call(kernel, outs, in_specs, scratch=()):
    return pl.pallas_call(
        kernel,
        out_shape=outs,
        in_specs=in_specs,
        out_specs=vmem(len(outs)) if isinstance(outs, list) else vmem(1)[0],
        scratch_shapes=list(scratch),
        compiler_params=pltpu.CompilerParams(vmem_limit_bytes=32 * 1024 * 1024),
        interpret=INTERPRET,
    )


def local(blended, estimate, neighbour_sources, partner_lags, threshold_level):
    lags = jnp.pad(partner_lags.reshape(-1), (0, 32))
    lags = lax.all_to_all(jnp.broadcast_to(lags, (DEVS, 128)), "shot", 0, 0, tiled=True)
    send = call(
        blend_kernel,
        jax.ShapeDtypeStruct((DEVS * 24, 128), jnp.bfloat16),
        [smem()] + vmem(2) + [pl.BlockSpec(memory_space=pl.ANY)],
        [
            pltpu.VMEM((BLOCK, CHANS, SAMPLES), jnp.float32),
            pltpu.VMEM((20 * CHANS * STEP + 16, 128), jnp.float32),
            pltpu.VMEM((44 * CHANS * STEP + 16, 128), jnp.float32),
            pltpu.VMEM((2048, 128), jnp.float32),
            pltpu.VMEM((DEVS, 24, 128), jnp.float32),
            pltpu.VMEM((SAMPLES, SAMPLES), jnp.bfloat16),
            pltpu.SemaphoreType.DMA,
        ],
    )(lags, blended, estimate, time_table())
    columns = lax.all_to_all(send.reshape(DEVS, 24, 128), "shot", 0, 0, tiled=True).reshape(DEVS * 24, 128)
    others = lax.axis_size("chan")
    spec, peak = call(
        forward_kernel,
        [jax.ShapeDtypeStruct((512, 128), jnp.float32), jax.ShapeDtypeStruct((others, 8, 128), jnp.float32)],
        vmem(4),
        [pltpu.VMEM((512, 128), jnp.float32)],
    )(columns, place_table(), twiddles(), block_table(-1))
    peaks = lax.all_to_all(peak, "chan", 0, 0, tiled=True)
    back = call(
        backward_kernel,
        jax.ShapeDtypeStruct((512, 128), jnp.bfloat16),
        [smem()] + vmem(5),
        [pltpu.VMEM((512, 128), jnp.float32)],
    )(threshold_level, spec, peaks, place_table(), twiddles(), block_table(1))
    arrived = lax.all_to_all(back.reshape(DEVS, 8, 128), "shot", 0, 0, tiled=True).reshape(512, 128)
    return call(
        time_back_kernel,
        jax.ShapeDtypeStruct((BLOCK, CHANS, SAMPLES), jnp.float32),
        vmem(2),
    )(arrived, time_back_table())


def solution(mesh):
    shots = P("shot", "chan", None)
    return jax.shard_map(
        local,
        mesh=mesh,
        in_specs=(shots, shots, P("shot", None), P("shot", None), P()),
        out_specs=shots,
        check_vma=False,
    )
```

```python
import jax
import jax.numpy as jnp
import numpy as np
from jax import lax
from jax.experimental import pallas as pl
from jax.experimental.pallas import tpu as pltpu
from jax.sharding import PartitionSpec as P

SHOTS, SAMPLES, FREQS = 1024, 1024, 512
DEVS, BLOCK, CHANS = 64, 16, 4
STEP = 24
INTERPRET = False


def time_table():
    t = np.arange(SAMPLES)[None, :]
    k = np.arange(FREQS)[:, None]
    phase = 2 * np.pi * ((t * k) % SAMPLES) / SAMPLES
    return (np.concatenate([np.cos(phase), -np.sin(phase)], 0) / 32).astype(jnp.bfloat16)


def time_back_table():
    t = np.arange(SAMPLES)[None, :]
    k = np.arange(FREQS)[:, None]
    phase = 2 * np.pi * ((t * k) % SAMPLES) / SAMPLES
    weight = np.where(k == 0, 1.0, 2.0) / 32
    return np.concatenate([weight * np.cos(phase), -weight * np.sin(phase)], 0).astype(jnp.bfloat16)


def place_table():
    phase = 2 * np.pi * (np.arange(64)[:, None] * np.arange(64)[None, :] % 64) / 64
    return np.concatenate([np.cos(phase), np.sin(phase)], 0).astype(jnp.bfloat16)


def twiddles():
    phase = 2 * np.pi * np.arange(64)[:, None] * np.arange(BLOCK)[None, :] / SHOTS
    cos, sin = np.tile(np.cos(phase), (1, 8)), np.tile(np.sin(phase), (1, 8))
    sin[:, 64:] *= -1
    return np.concatenate([cos, sin], 1).astype(np.float32)


def block_table(sign):
    out = np.zeros((2, CHANS, 16, 2, CHANS, 16), np.float64)
    phase = 2 * np.pi * (np.arange(16)[:, None] * np.arange(16)[None, :] % 16) / 16
    for c in range(CHANS):
        out[0, c, :, 0, c, :] = np.cos(phase)
        out[1, c, :, 1, c, :] = np.cos(phase)
        out[0, c, :, 1, c, :] = sign * np.sin(phase)
        out[1, c, :, 0, c, :] = -sign * np.sin(phase)
    return (out.reshape(128, 128) / 32).astype(jnp.bfloat16)


def lane_ids(*shape):
    return lax.broadcasted_iota(jnp.int32, (*shape, 128), len(shape))


def swapped(value):
    return pltpu.roll(value, 64, value.ndim - 1)


def base(row, c):
    return (row * CHANS + c) * STEP + 16


def res_row(side, n):
    return side * 22 + n + 3


def place_of(side, n):
    low = 128 + (14 if side == 0 else 12) + n + 2
    high = 128 + (0 if side == 0 else 2) + n - 16
    return jnp.where(n < 0, low, jnp.where(n > 15, high, side * 64 + n))


def add_shifted(total, ref, first, lag, lanes):
    turn = lag & 127
    keep = lanes < 128 - turn
    first = first - (lag >> 7)
    for c in range(CHANS):
        here = ref[pl.ds(first + c * STEP, 8), :]
        before = ref[pl.ds(first + c * STEP - 1, 8), :]
        moved = pltpu.roll(jnp.where(keep, here, before), turn, 1)
        total[c] = moved if total[c] is None else total[c] + moved


def fleet_of(shot):
    return ((shot + 1) >> 9) & 1


def residual_kernel(lag_ref, dat_ref, est_ref, res, part, tmp, est):
    place = lax.axis_index("shot")
    est[...] = jnp.zeros_like(est)
    res[...] = jnp.zeros_like(res)
    part[1024:, :] = jnp.zeros((512, 128), jnp.float32)
    tmp[...] = est_ref[...].astype(jnp.float32)
    for c in range(CHANS):
        for u in range(8):
            columns = slice(128 * u, 128 * u + 128)
            old = tmp[:, c, columns]
            est[pl.ds(base(2, c) + u, BLOCK, stride=CHANS * STEP), :] = old
            res[pl.ds(base(3, c) + u, BLOCK, stride=CHANS * STEP), :] = dat_ref[:, c, columns] - old
    lanes = lane_ids(8)

    @pl.loop(0, BLOCK + 2)
    def _(step):
        n = step - 1
        for side in range(2):
            total = [None] * CHANS
            for ahead in (-1, 1) if side == 0 else (-1, 0, 1):
                m = jnp.clip(n + ahead, 0, BLOCK - 1)
                fleet = fleet_of(BLOCK * place + m)
                lag = -lag_ref[m * 6 + 3 * (fleet ^ side) + 1 - ahead]
                add_shifted(total, est, base(n + ahead + 2, 0), lag, lanes)
            for c in range(CHANS):
                rows = pl.ds(base(res_row(side, n), c), 8)
                value = -total[c] if side else res[rows, :] - total[c]
                res[rows, :] = value
                value = 0.25 * value
                if side == 0:
                    value = value + est[pl.ds(base(n + 2, c), 8), :]
                part[pl.ds((place_of(side, n) + c * BLOCK) * 8, 8), :] = value


def blend_kernel(lag_ref, res, part, table_hbm, out_ref, upd, acc, table, sem):
    copy = pltpu.make_async_copy(table_hbm, table, sem)
    copy.start()
    place = lax.axis_index("shot")
    upd[1024:, :] = jnp.zeros((1024, 128), jnp.float32)
    lanes = lane_ids(8)

    @pl.loop(0, BLOCK + 4)
    def _(step):
        n = step - 2
        for side in range(2):
            shot = (512 * side + BLOCK * place + n + SHOTS) & (SHOTS - 1)
            fleet = fleet_of(shot)
            total = [None] * CHANS
            for flip, ahead in ((0, -1), (0, 1), (1, -1), (1, 0), (1, 1)):
                lag = lag_ref[shot >> 4, (shot & 15) * 6 + 3 * (fleet ^ flip) + 1 + ahead]
                add_shifted(total, res, base(res_row(side ^ flip, n + ahead), 0), lag, lanes)
            for c in range(CHANS):
                rows = pl.ds((place_of(side, n) + c * BLOCK) * 8, 8)
                upd[rows, :] = part[rows, :] + 0.25 * total[c]

    rows = jnp.concatenate([upd[pl.ds(u, 256, stride=8), :] for u in range(8)], 1).astype(jnp.bfloat16)
    copy.wait()
    rims = None
    for ri in range(2):
        product = lax.dot_general(
            table[512 * ri : 512 * ri + 512, :],
            rows,
            (((1,), (1,)), ((), ())),
            preferred_element_type=jnp.float32,
        )
        acc[:, 8 * ri : 8 * ri + 8, :] = product[:, :128].reshape(DEVS, 8, 128)
        rims = product[:, 128:] if rims is None else rims + swapped(product[:, 128:])
    acc[:, 16:24, :] = rims.reshape(DEVS, 8, 128)
    out_ref[...] = acc[...].reshape(DEVS * 24, 128).astype(jnp.bfloat16)


def forward_kernel(level_ref, x_ref, place_ref, turn_ref, block_ref, spec_ref, limit_ref, tmp):
    x = x_ref[...].astype(jnp.float32).reshape(DEVS, 24, 128)
    real, imag, rims = x[:, :8], x[:, 8:16], x[:, 16:]

    def ahead(value, count):
        return jnp.concatenate([value[count:], value[:count]], 0)

    def lane_roll(value, shift):
        return pltpu.roll(value.reshape(512, 128), shift, 1).reshape(DEVS, 8, 128)

    lanes = lane_ids(DEVS, 8)
    within = lanes & 15
    total = jnp.where(
        lanes < 64,
        real + lane_roll(ahead(real, 32), 64),
        lane_roll(imag, 64) + ahead(imag, 32),
    )
    far = ahead(rims, 32)
    rims = rims + jnp.where(within < 8, lane_roll(far, 126), lane_roll(far, 2))
    total = total + jnp.where(within < 2, ahead(rims, 63), jnp.where(within >= 14, ahead(rims, 1), 0.0))
    tmp[...] = total.reshape(512, 128)
    rhs = jnp.concatenate([tmp[pl.ds(kk, 64, stride=8), :] for kk in range(8)], 1).astype(jnp.bfloat16)
    product = jnp.dot(place_ref[...], rhs, preferred_element_type=jnp.float32)
    cos, sin = turn_ref[:, :128], turn_ref[:, 128:]
    half = lane_ids(64) < 64
    turned = []
    for kk in range(8):
        columns = slice(128 * kk, 128 * kk + 128)
        other = swapped(product[64:, columns])
        value = product[:64, columns] + jnp.where(half, other, -other)
        turned.append((value * cos + swapped(value) * sin).astype(jnp.bfloat16))
    spec = jnp.dot(jnp.concatenate(turned, 0), block_ref[...], preferred_element_type=jnp.float32)
    spec_ref[...] = spec
    square = spec * spec
    square = square + swapped(square)
    peak = jnp.concatenate(
        [jnp.max(square[64 * kk : 64 * kk + 64], axis=0, keepdims=True) for kk in range(8)], 0
    )
    for shift in (1, 2, 4, 8, 16, 32):
        peak = jnp.maximum(peak, pltpu.roll(peak, shift, 1))
    limit = level_ref[0].astype(jnp.float32) * (1 / 64) * (jnp.sqrt(peak) + 1e-6)
    limit_ref[...] = jnp.broadcast_to(limit[None], limit_ref.shape)


def backward_kernel(spec_ref, limit_ref, place_ref, turn_ref, block_ref, out_ref, tmp):
    limit = jnp.max(limit_ref[...], axis=0)
    shrunk = []
    for kk in range(8):
        value = spec_ref[64 * kk : 64 * kk + 64, :]
        square = value * value
        size = jnp.sqrt(square + swapped(square))
        bound = limit[kk : kk + 1]
        factor = jnp.maximum(size - bound, 0.0) / jnp.maximum(size, bound)
        shrunk.append((value * factor).astype(jnp.bfloat16))
    product = jnp.dot(jnp.concatenate(shrunk, 0), block_ref[...], preferred_element_type=jnp.float32)
    cos, sin = turn_ref[:, :128], turn_ref[:, 128:]
    turned = []
    for kk in range(8):
        value = product[64 * kk : 64 * kk + 64]
        turned.append((value * cos - swapped(value) * sin).astype(jnp.bfloat16))
    product = jnp.dot(place_ref[...], jnp.concatenate(turned, 1), preferred_element_type=jnp.float32)
    half = lane_ids(64) < 64
    for kk in range(8):
        columns = slice(128 * kk, 128 * kk + 128)
        other = swapped(product[64:, columns])
        tmp[pl.ds(kk, 64, stride=8), :] = product[:64, columns] - jnp.where(half, other, -other)
    out_ref[...] = tmp[...].astype(jnp.bfloat16)


def time_back_kernel(x_ref, table_ref, out_ref):
    turned = x_ref[...].astype(jnp.float32).T.astype(jnp.bfloat16)
    left = jnp.concatenate([turned[:64], turned[64:]], 1)
    for n in range(4):
        columns = slice(256 * n, 256 * n + 256)
        product = jnp.dot(left, table_ref[:, columns], preferred_element_type=jnp.float32)
        for c in range(CHANS):
            out_ref[:, c, columns] = product[BLOCK * c : BLOCK * c + BLOCK]


def vmem(count):
    return [pl.BlockSpec(memory_space=pltpu.VMEM)] * count


def smem():
    return pl.BlockSpec(memory_space=pltpu.SMEM)


def call(kernel, outs, in_specs, scratch=(), cost=None):
    return pl.pallas_call(
        kernel,
        out_shape=outs,
        in_specs=in_specs,
        out_specs=vmem(len(outs)) if isinstance(outs, list) else vmem(1)[0],
        scratch_shapes=list(scratch),
        compiler_params=pltpu.CompilerParams(vmem_limit_bytes=32 * 1024 * 1024),
        cost_estimate=cost,
        interpret=INTERPRET,
    )


def local(blended, estimate, neighbour_sources, partner_lags, threshold_level):
    lags = jnp.pad(partner_lags.reshape(-1), (0, 32))
    all_lags = lax.all_to_all(jnp.broadcast_to(lags, (DEVS, 128)), "shot", 0, 0, tiled=True)
    res, part = call(
        residual_kernel,
        [
            jax.ShapeDtypeStruct((44 * CHANS * STEP + 16, 128), jnp.float32),
            jax.ShapeDtypeStruct((192 * 8, 128), jnp.float32),
        ],
        [smem()] + vmem(2),
        [
            pltpu.VMEM((BLOCK, CHANS, SAMPLES), jnp.float32),
            pltpu.VMEM((20 * CHANS * STEP + 16, 128), jnp.float32),
        ],
        pl.CostEstimate(flops=4_000_000, bytes_accessed=16_000_000, transcendentals=0),
    )(lags, blended, estimate)
    send = call(
        blend_kernel,
        jax.ShapeDtypeStruct((DEVS * 24, 128), jnp.bfloat16),
        [smem()] + vmem(2) + [pl.BlockSpec(memory_space=pl.ANY)],
        [
            pltpu.VMEM((2048, 128), jnp.float32),
            pltpu.VMEM((DEVS, 24, 128), jnp.float32),
            pltpu.VMEM((SAMPLES, SAMPLES), jnp.bfloat16),
            pltpu.SemaphoreType.DMA,
        ],
    )(all_lags, res, part, time_table())
    columns = lax.all_to_all(send.reshape(DEVS, 24, 128), "shot", 0, 0, tiled=True).reshape(DEVS * 24, 128)
    others = lax.axis_size("chan")
    spec, limit = call(
        forward_kernel,
        [jax.ShapeDtypeStruct((512, 128), jnp.float32), jax.ShapeDtypeStruct((others, 8, 128), jnp.float32)],
        [smem()] + vmem(4),
        [pltpu.VMEM((512, 128), jnp.float32)],
    )(threshold_level, columns, place_table(), twiddles(), block_table(-1))
    limits = lax.all_to_all(limit, "chan", 0, 0, tiled=True)
    back = call(
        backward_kernel,
        jax.ShapeDtypeStruct((512, 128), jnp.bfloat16),
        vmem(5),
        [pltpu.VMEM((512, 128), jnp.float32)],
    )(spec, limits, place_table(), twiddles(), block_table(1))
    arrived = lax.all_to_all(back.reshape(DEVS, 8, 128), "shot", 0, 0, tiled=True).reshape(512, 128)
    return call(
        time_back_kernel,
        jax.ShapeDtypeStruct((BLOCK, CHANS, SAMPLES), jnp.float32),
        vmem(2),
    )(arrived, time_back_table())


def solution(mesh):
    shots = P("shot", "chan", None)
    return jax.shard_map(
        local,
        mesh=mesh,
        in_specs=(shots, shots, P("shot", None), P("shot", None), P()),
        out_specs=shots,
        check_vma=False,
    )
```

```python
import jax
import jax.numpy as jnp
import numpy as np
from jax import lax
from jax.experimental import pallas as pl
from jax.experimental.pallas import tpu as pltpu
from jax.sharding import PartitionSpec as P

SHOTS, SAMPLES, FREQS = 1024, 1024, 512
DEVS, BLOCK, CHANS = 64, 16, 4
STEP = 24
INTERPRET = False


def half_phases(parity):
    k = 2 * np.arange(FREQS // 2)[:, None] + parity
    t = np.arange(SAMPLES // 2)[None, :]
    return k, 2 * np.pi * ((t * k) % SAMPLES) / SAMPLES


def time_table():
    parts = []
    for parity in range(2):
        _, phase = half_phases(parity)
        parts += [np.cos(phase) / 32, -np.sin(phase) / 32]
    return np.concatenate(parts, 0).astype(jnp.bfloat16)


def time_back_table():
    parts = []
    for parity in range(2):
        k, phase = half_phases(parity)
        weight = np.where(k == 0, 1.0, 2.0) / 32
        parts += [weight * np.cos(phase), -weight * np.sin(phase)]
    return np.concatenate(parts, 0).astype(jnp.bfloat16)


def place_table():
    phase = 2 * np.pi * (np.arange(64)[:, None] * np.arange(64)[None, :] % 64) / 64
    return np.concatenate([np.cos(phase), np.sin(phase)], 0).astype(jnp.bfloat16)


def twiddles():
    phase = 2 * np.pi * np.arange(64)[:, None] * np.arange(BLOCK)[None, :] / SHOTS
    cos, sin = np.tile(np.cos(phase), (1, 8)), np.tile(np.sin(phase), (1, 8))
    sin[:, 64:] *= -1
    return np.concatenate([cos, sin], 1).astype(np.float32)


def block_table(sign):
    out = np.zeros((2, CHANS, 16, 2, CHANS, 16), np.float64)
    phase = 2 * np.pi * (np.arange(16)[:, None] * np.arange(16)[None, :] % 16) / 16
    for c in range(CHANS):
        out[0, c, :, 0, c, :] = np.cos(phase)
        out[1, c, :, 1, c, :] = np.cos(phase)
        out[0, c, :, 1, c, :] = sign * np.sin(phase)
        out[1, c, :, 0, c, :] = -sign * np.sin(phase)
    return (out.reshape(128, 128) / 32).astype(jnp.bfloat16)


def lane_ids(*shape):
    return lax.broadcasted_iota(jnp.int32, (*shape, 128), len(shape))


def swapped(value):
    return pltpu.roll(value, 64, value.ndim - 1)


def base(row, c):
    return (row * CHANS + c) * STEP + 16


def res_row(side, n):
    return side * 22 + n + 3


def place_of(side, n):
    low = 128 + (14 if side == 0 else 12) + n + 2
    high = 128 + (0 if side == 0 else 2) + n - 16
    return jnp.where(n < 0, low, jnp.where(n > 15, high, side * 64 + n))


def add_shifted(total, ref, first, lag, lanes):
    turn = lag & 127
    keep = lanes < 128 - turn
    first = first - (lag >> 7)
    for c in range(CHANS):
        here = ref[pl.ds(first + c * STEP, 8), :]
        before = ref[pl.ds(first + c * STEP - 1, 8), :]
        moved = pltpu.roll(jnp.where(keep, here, before), turn, 1)
        total[c] = moved if total[c] is None else total[c] + moved


def fleet_of(shot):
    return ((shot + 1) >> 9) & 1


def lag_kernel(lag_ref, out_ref):
    own = jnp.pad(lag_ref[...], ((0, 0), (0, 128 - BLOCK)))
    row = own[0:1]
    for slot in range(1, 6):
        row = row + pltpu.roll(own[slot : slot + 1], BLOCK * slot, 1)
    out_ref[...] = jnp.broadcast_to(row, out_ref.shape)


def residual_kernel(level_ref, lag_ref, dat_ref, est_ref, res, part, level_out, tmp, est):
    place = lax.axis_index("shot")
    level_out[...] = jnp.full((8, 128), level_ref[0].astype(jnp.float32) * (1 / 64))
    est[...] = jnp.zeros_like(est)
    res[...] = jnp.zeros_like(res)
    part[1024:, :] = jnp.zeros((512, 128), jnp.float32)
    tmp[...] = est_ref[...].astype(jnp.float32)
    for c in range(CHANS):
        for u in range(8):
            columns = slice(128 * u, 128 * u + 128)
            old = tmp[:, c, columns]
            est[pl.ds(base(2, c) + u, BLOCK, stride=CHANS * STEP), :] = old
            res[pl.ds(base(3, c) + u, BLOCK, stride=CHANS * STEP), :] = dat_ref[:, c, columns] - old
    lanes = lane_ids(8)

    @pl.loop(0, BLOCK + 2, unroll=2)
    def _(step):
        n = step - 1
        for side in range(2):
            total = [None] * CHANS
            for ahead in (-1, 1) if side == 0 else (-1, 0, 1):
                m = jnp.clip(n + ahead, 0, BLOCK - 1)
                fleet = fleet_of(BLOCK * place + m)
                lag = -lag_ref[0, (3 * (fleet ^ side) + 1 - ahead) * BLOCK + m]
                add_shifted(total, est, base(n + ahead + 2, 0), lag, lanes)
            for c in range(CHANS):
                rows = pl.ds(base(res_row(side, n), c), 8)
                value = -total[c] if side else res[rows, :] - total[c]
                res[rows, :] = value
                value = 0.25 * value
                if side == 0:
                    value = value + est[pl.ds(base(n + 2, c), 8), :]
                part[pl.ds((place_of(side, n) + c * BLOCK) * 8, 8), :] = value


def blend_kernel(lag_ref, res, part, table, out_ref, upd, acc):
    place = lax.axis_index("shot")
    upd[1024:, :] = jnp.zeros((1024, 128), jnp.float32)
    lanes = lane_ids(8)

    @pl.loop(0, BLOCK + 4, unroll=4)
    def _(step):
        n = step - 2
        for side in range(2):
            shot = (512 * side + BLOCK * place + n + SHOTS) & (SHOTS - 1)
            fleet = fleet_of(shot)
            total = [None] * CHANS
            for flip, ahead in ((0, -1), (0, 1), (1, -1), (1, 0), (1, 1)):
                lag = lag_ref[shot >> 4, (3 * (fleet ^ flip) + 1 + ahead) * BLOCK + (shot & 15)]
                add_shifted(total, res, base(res_row(side ^ flip, n + ahead), 0), lag, lanes)
            for c in range(CHANS):
                rows = pl.ds((place_of(side, n) + c * BLOCK) * 8, 8)
                upd[rows, :] = part[rows, :] + 0.25 * total[c]

    octaves = [upd[pl.ds(u, 256, stride=8), :] for u in range(8)]
    for parity in range(2):
        rows = [octaves[u] - octaves[u + 4] if parity else octaves[u] + octaves[u + 4] for u in range(4)]
        product = lax.dot_general(
            table[512 * parity : 512 * parity + 512, :],
            jnp.concatenate(rows, 1).astype(jnp.bfloat16),
            (((1,), (1,)), ((), ())),
            preferred_element_type=jnp.float32,
        )
        real, imag = product[:256], product[256:]
        for at, value in ((0, real[:, :128]), (8, imag[:, :128]), (16, real[:, 128:] + swapped(imag[:, 128:]))):
            acc[:, parity, at : at + 8, :] = value.reshape(DEVS // 2, 8, 128)
    out_ref[...] = acc[...].reshape(DEVS * 24, 128).astype(jnp.bfloat16)


def forward_kernel(level_ref, x_ref, place_ref, turn_ref, block_ref, spec_ref, limit_ref, tmp):
    x = x_ref[...].astype(jnp.float32).reshape(DEVS, 24, 128)
    real, imag, rims = x[:, :8], x[:, 8:16], x[:, 16:]

    def ahead(value, count):
        return jnp.concatenate([value[count:], value[:count]], 0)

    def lane_roll(value, shift):
        return pltpu.roll(value.reshape(512, 128), shift, 1).reshape(DEVS, 8, 128)

    lanes = lane_ids(DEVS, 8)
    within = lanes & 15
    total = jnp.where(
        lanes < 64,
        real + lane_roll(ahead(real, 32), 64),
        lane_roll(imag, 64) + ahead(imag, 32),
    )
    far = ahead(rims, 32)
    rims = rims + jnp.where(within < 8, lane_roll(far, 126), lane_roll(far, 2))
    total = total + jnp.where(within < 2, ahead(rims, 63), jnp.where(within >= 14, ahead(rims, 1), 0.0))
    tmp[...] = total.reshape(512, 128)
    rhs = jnp.concatenate([tmp[pl.ds(kk, 64, stride=8), :] for kk in range(8)], 1).astype(jnp.bfloat16)
    product = jnp.dot(place_ref[...], rhs, preferred_element_type=jnp.float32)
    cos, sin = turn_ref[:, :128], turn_ref[:, 128:]
    half = lane_ids(64) < 64
    turned = []
    for kk in range(8):
        columns = slice(128 * kk, 128 * kk + 128)
        other = swapped(product[64:, columns])
        value = product[:64, columns] + jnp.where(half, other, -other)
        turned.append((value * cos + swapped(value) * sin).astype(jnp.bfloat16))
    spec = jnp.dot(jnp.concatenate(turned, 0), block_ref[...], preferred_element_type=jnp.float32)
    spec_ref[...] = spec
    square = spec * spec
    square = square + swapped(square)
    peak = jnp.concatenate(
        [jnp.max(square[64 * kk : 64 * kk + 64], axis=0, keepdims=True) for kk in range(8)], 0
    )
    for shift in (1, 2, 4, 8, 16, 32):
        peak = jnp.maximum(peak, pltpu.roll(peak, shift, 1))
    limit = level_ref[...] * (jnp.sqrt(peak) + 1e-6)
    limit_ref[...] = jnp.broadcast_to(limit[None], limit_ref.shape)


def backward_kernel(spec_ref, limit_ref, place_ref, turn_ref, block_ref, out_ref, tmp):
    limit = jnp.max(limit_ref[...], axis=0)
    shrunk = []
    for kk in range(8):
        value = spec_ref[64 * kk : 64 * kk + 64, :]
        square = value * value
        size = jnp.sqrt(square + swapped(square))
        bound = limit[kk : kk + 1]
        factor = jnp.maximum(size - bound, 0.0) / jnp.maximum(size, bound)
        shrunk.append((value * factor).astype(jnp.bfloat16))
    product = jnp.dot(jnp.concatenate(shrunk, 0), block_ref[...], preferred_element_type=jnp.float32)
    cos, sin = turn_ref[:, :128], turn_ref[:, 128:]
    turned = []
    for kk in range(8):
        value = product[64 * kk : 64 * kk + 64]
        turned.append((value * cos - swapped(value) * sin).astype(jnp.bfloat16))
    product = jnp.dot(place_ref[...], jnp.concatenate(turned, 1), preferred_element_type=jnp.float32)
    half = lane_ids(64) < 64
    for kk in range(8):
        columns = slice(128 * kk, 128 * kk + 128)
        other = swapped(product[64:, columns])
        tmp[pl.ds(kk, 64, stride=8), :] = product[:64, columns] - jnp.where(half, other, -other)
    out_ref[...] = tmp[...].astype(jnp.bfloat16)


def time_back_kernel(x_ref, table_ref, out_ref):
    x = x_ref[...].astype(jnp.float32).reshape(DEVS // 2, 2, 8, 128)
    halves = []
    for parity in range(2):
        turned = x[:, parity].reshape(256, 128).T.astype(jnp.bfloat16)
        left = jnp.concatenate([turned[:64], turned[64:]], 1)
        table = table_ref[512 * parity : 512 * parity + 512, :]
        halves.append(jnp.dot(left, table, preferred_element_type=jnp.float32))
    for half, value in enumerate((halves[0] + halves[1], halves[0] - halves[1])):
        for c in range(CHANS):
            out_ref[:, c, 512 * half : 512 * half + 512] = value[BLOCK * c : BLOCK * c + BLOCK]


def vmem(count):
    return [pl.BlockSpec(memory_space=pltpu.VMEM)] * count


def smem():
    return pl.BlockSpec(memory_space=pltpu.SMEM)


def call(kernel, outs, in_specs, scratch=(), cost=None):
    return pl.pallas_call(
        kernel,
        out_shape=outs,
        in_specs=in_specs,
        out_specs=vmem(len(outs)) if isinstance(outs, list) else vmem(1)[0],
        scratch_shapes=list(scratch),
        compiler_params=pltpu.CompilerParams(vmem_limit_bytes=8 * 1024 * 1024),
        cost_estimate=cost,
        interpret=INTERPRET,
    )


def local(blended, estimate, neighbour_sources, partner_lags, threshold_level):
    own_lags = call(lag_kernel, jax.ShapeDtypeStruct((DEVS, 128), jnp.int32), vmem(1))(partner_lags.T)
    all_lags = lax.all_to_all(own_lags, "shot", 0, 0, tiled=True)
    res, part, level = call(
        residual_kernel,
        [
            jax.ShapeDtypeStruct((44 * CHANS * STEP + 16, 128), jnp.float32),
            jax.ShapeDtypeStruct((192 * 8, 128), jnp.float32),
            jax.ShapeDtypeStruct((8, 128), jnp.float32),
        ],
        [smem()] * 2 + vmem(2),
        [
            pltpu.VMEM((BLOCK, CHANS, SAMPLES), jnp.float32),
            pltpu.VMEM((20 * CHANS * STEP + 16, 128), jnp.float32),
        ],
        pl.CostEstimate(flops=4_000_000, bytes_accessed=16_000_000, transcendentals=0),
    )(threshold_level, own_lags, blended, estimate)
    send = call(
        blend_kernel,
        jax.ShapeDtypeStruct((DEVS * 24, 128), jnp.bfloat16),
        [smem()] + vmem(3),
        [pltpu.VMEM((2048, 128), jnp.float32), pltpu.VMEM((DEVS // 2, 2, 24, 128), jnp.float32)],
    )(all_lags, res, part, time_table())
    columns = lax.all_to_all(send.reshape(DEVS, 24, 128), "shot", 0, 0, tiled=True).reshape(DEVS * 24, 128)
    others = lax.axis_size("chan")
    spec, limit = call(
        forward_kernel,
        [jax.ShapeDtypeStruct((512, 128), jnp.float32), jax.ShapeDtypeStruct((others, 8, 128), jnp.float32)],
        vmem(5),
        [pltpu.VMEM((512, 128), jnp.float32)],
    )(level, columns, place_table(), twiddles(), block_table(-1))
    limits = lax.all_to_all(limit, "chan", 0, 0, tiled=True)
    back = call(
        backward_kernel,
        jax.ShapeDtypeStruct((512, 128), jnp.bfloat16),
        vmem(5),
        [pltpu.VMEM((512, 128), jnp.float32)],
    )(spec, limits, place_table(), twiddles(), block_table(1))
    arrived = lax.all_to_all(back.reshape(DEVS, 8, 128), "shot", 0, 0, tiled=True).reshape(512, 128)
    return call(
        time_back_kernel,
        jax.ShapeDtypeStruct((BLOCK, CHANS, SAMPLES), jnp.float32),
        vmem(2),
    )(arrived, time_back_table())


def solution(mesh):
    shots = P("shot", "chan", None)
    return jax.shard_map(
        local,
        mesh=mesh,
        in_specs=(shots, shots, P("shot", None), P("shot", None), P()),
        out_specs=shots,
        check_vma=False,
    )
```

```python
import jax
import jax.numpy as jnp
import numpy as np
from jax import lax
from jax.experimental import pallas as pl
from jax.experimental.pallas import tpu as pltpu
from jax.sharding import PartitionSpec as P

SHOTS, SAMPLES, FREQS = 1024, 1024, 512
DEVS, BLOCK, CHANS = 64, 16, 4
STEP = 24
INTERPRET = False


def half_phases(parity):
    k = 2 * np.arange(FREQS // 2)[:, None] + parity
    t = np.arange(SAMPLES // 2)[None, :]
    return k, 2 * np.pi * ((t * k) % SAMPLES) / SAMPLES


def time_table():
    parts = []
    for parity in range(2):
        _, phase = half_phases(parity)
        parts += [np.cos(phase) / 32, -np.sin(phase) / 32]
    return np.concatenate(parts, 0).astype(jnp.bfloat16)


def time_back_table():
    parts = []
    for parity in range(2):
        k, phase = half_phases(parity)
        weight = np.where(k == 0, 1.0, 2.0) / 32
        parts += [weight * np.cos(phase), -weight * np.sin(phase)]
    return np.concatenate(parts, 0).astype(jnp.bfloat16)


def place_table():
    phase = 2 * np.pi * (np.arange(64)[:, None] * np.arange(64)[None, :] % 64) / 64
    return np.concatenate([np.cos(phase), np.sin(phase)], 0).astype(jnp.bfloat16)


def twiddles():
    phase = 2 * np.pi * np.arange(64)[:, None] * np.arange(BLOCK)[None, :] / SHOTS
    cos, sin = np.tile(np.cos(phase), (1, 8)), np.tile(np.sin(phase), (1, 8))
    sin[:, 64:] *= -1
    return np.concatenate([cos, sin], 1).astype(np.float32)


def block_table(sign):
    out = np.zeros((2, CHANS, 16, 2, CHANS, 16), np.float64)
    phase = 2 * np.pi * (np.arange(16)[:, None] * np.arange(16)[None, :] % 16) / 16
    for c in range(CHANS):
        out[0, c, :, 0, c, :] = np.cos(phase)
        out[1, c, :, 1, c, :] = np.cos(phase)
        out[0, c, :, 1, c, :] = sign * np.sin(phase)
        out[1, c, :, 0, c, :] = -sign * np.sin(phase)
    return (out.reshape(128, 128) / 32).astype(jnp.bfloat16)


def lane_ids(*shape):
    return lax.broadcasted_iota(jnp.int32, (*shape, 128), len(shape))


def swapped(value):
    return pltpu.roll(value, 64, value.ndim - 1)


def base(row, c):
    return (row * CHANS + c) * STEP + 16


def res_row(side, n):
    return side * 22 + n + 3


def place_of(side, n):
    low = 128 + (14 if side == 0 else 12) + n + 2
    high = 128 + (0 if side == 0 else 2) + n - 16
    return jnp.where(n < 0, low, jnp.where(n > 15, high, side * 64 + n))


def add_shifted(total, ref, first, lag, lanes):
    turn = lag & 127
    keep = lanes < 128 - turn
    first = first - (lag >> 7)
    for c in range(CHANS):
        here = ref[pl.ds(first + c * STEP, 8), :]
        before = ref[pl.ds(first + c * STEP - 1, 8), :]
        moved = pltpu.roll(jnp.where(keep, here, before), turn, 1)
        total[c] = moved if total[c] is None else total[c] + moved


def fleet_of(shot):
    return ((shot + 1) >> 9) & 1


def residual_kernel(level_ref, all_lags, dat_ref, est_ref, res, part, level_out, tmp, est, lag_ref, sem):
    copy = pltpu.make_async_copy(all_lags.at[0], lag_ref, sem)
    copy.start()
    place = lax.axis_index("shot")
    level_out[...] = jnp.full((8, 128), level_ref[0].astype(jnp.float32) * (1 / 64))
    est[...] = jnp.zeros_like(est)
    res[...] = jnp.zeros_like(res)
    part[1024:, :] = jnp.zeros((512, 128), jnp.float32)
    tmp[...] = est_ref[...].astype(jnp.float32)
    for c in range(CHANS):
        for u in range(8):
            columns = slice(128 * u, 128 * u + 128)
            old = tmp[:, c, columns]
            est[pl.ds(base(2, c) + u, BLOCK, stride=CHANS * STEP), :] = old
            res[pl.ds((CHANS + c) * 8 + u, BLOCK, stride=CHANS * 8), :] = dat_ref[:, c, columns] - old
    lanes = lane_ids(8)
    copy.wait()

    @pl.loop(0, BLOCK + 2, unroll=3)
    def _(step):
        n = step - 1
        for side in range(2):
            total = [None] * CHANS
            for ahead in (-1, 1) if side == 0 else (-1, 0, 1):
                m = jnp.clip(n + ahead, 0, BLOCK - 1)
                fleet = fleet_of(BLOCK * place + m)
                lag = -lag_ref[(3 * (fleet ^ side) + 1 - ahead) * BLOCK + m]
                add_shifted(total, est, base(n + ahead + 2, 0), lag, lanes)
            for c in range(CHANS):
                rows = pl.ds(((side * 18 + step) * CHANS + c) * 8, 8)
                value = -total[c] if side else res[rows, :] - total[c]
                res[rows, :] = value
                value = 0.25 * value
                if side == 0:
                    value = value + est[pl.ds(base(n + 2, c), 8), :]
                part[pl.ds((place_of(side, n) + c * BLOCK) * 8, 8), :] = value


def blend_kernel(all_lags, res_ref, part, out_ref, res, upd, lag_ref, sems):
    place = lax.axis_index("shot")
    copies = []
    for number in range(6):
        source = (place + number % 3 - 1 + 32 * (number // 3) + DEVS) & (DEVS - 1)
        copies.append(pltpu.make_async_copy(all_lags.at[source], lag_ref.at[number], sems.at[number]))
        copies[-1].start()
    upd[1024:, :] = jnp.zeros((1024, 128), jnp.float32)
    res[...] = jnp.zeros_like(res)
    for side in range(2):
        for row in range(18):
            for c in range(CHANS):
                at = ((side * 18 + row) * CHANS + c) * 8
                res[pl.ds(base(res_row(side, row - 1), c), 8), :] = res_ref[at : at + 8, :]
    lanes = lane_ids(8)
    for copy in copies:
        copy.wait()

    @pl.loop(0, BLOCK + 4, unroll=5)
    def _(step):
        n = step - 2
        for side in range(2):
            shot = (512 * side + BLOCK * place + n + SHOTS) & (SHOTS - 1)
            fleet = fleet_of(shot)
            total = [None] * CHANS
            for flip, ahead in ((0, -1), (0, 1), (1, -1), (1, 0), (1, 1)):
                lag = lag_ref[side * 3 + ((n + BLOCK) >> 4), (3 * (fleet ^ flip) + 1 + ahead) * BLOCK + (shot & 15)]
                add_shifted(total, res, base(res_row(side ^ flip, n + ahead), 0), lag, lanes)
            for c in range(CHANS):
                rows = pl.ds((place_of(side, n) + c * BLOCK) * 8, 8)
                upd[rows, :] = part[rows, :] + 0.25 * total[c]

    octaves = [upd[pl.ds(u, 256, stride=8), :] for u in range(8)]
    for parity in range(2):
        rows = [octaves[u] - octaves[u + 4] if parity else octaves[u] + octaves[u + 4] for u in range(4)]
        out_ref[256 * parity : 256 * parity + 256, :] = jnp.concatenate(rows, 1).astype(jnp.bfloat16)


def time_kernel(rows_ref, table, out_ref, acc):
    for parity in range(2):
        product = lax.dot_general(
            table[512 * parity : 512 * parity + 512, :],
            rows_ref[256 * parity : 256 * parity + 256, :],
            (((1,), (1,)), ((), ())),
            preferred_element_type=jnp.float32,
        )
        real, imag = product[:256], product[256:]
        for at, value in ((0, real[:, :128]), (8, imag[:, :128]), (16, real[:, 128:] + swapped(imag[:, 128:]))):
            acc[:, parity, at : at + 8, :] = value.reshape(DEVS // 2, 8, 128)
    out_ref[...] = acc[...].reshape(DEVS * 24, 128).astype(jnp.bfloat16)


def forward_kernel(level_ref, x_ref, place_ref, turn_ref, block_ref, spec_ref, limit_ref, tmp):
    x = x_ref[...].astype(jnp.float32).reshape(DEVS, 24, 128)
    real, imag, rims = x[:, :8], x[:, 8:16], x[:, 16:]

    def ahead(value, count):
        return jnp.concatenate([value[count:], value[:count]], 0)

    def lane_roll(value, shift):
        return pltpu.roll(value.reshape(512, 128), shift, 1).reshape(DEVS, 8, 128)

    lanes = lane_ids(DEVS, 8)
    within = lanes & 15
    total = jnp.where(
        lanes < 64,
        real + lane_roll(ahead(real, 32), 64),
        lane_roll(imag, 64) + ahead(imag, 32),
    )
    far = ahead(rims, 32)
    rims = rims + jnp.where(within < 8, lane_roll(far, 126), lane_roll(far, 2))
    total = total + jnp.where(within < 2, ahead(rims, 63), jnp.where(within >= 14, ahead(rims, 1), 0.0))
    tmp[...] = total.reshape(512, 128)
    rhs = jnp.concatenate([tmp[pl.ds(kk, 64, stride=8), :] for kk in range(8)], 1).astype(jnp.bfloat16)
    product = jnp.dot(place_ref[...], rhs, preferred_element_type=jnp.float32)
    cos, sin = turn_ref[:, :128], turn_ref[:, 128:]
    half = lane_ids(64) < 64
    turned = []
    for kk in range(8):
        columns = slice(128 * kk, 128 * kk + 128)
        other = swapped(product[64:, columns])
        value = product[:64, columns] + jnp.where(half, other, -other)
        turned.append((value * cos + swapped(value) * sin).astype(jnp.bfloat16))
    spec = jnp.dot(jnp.concatenate(turned, 0), block_ref[...], preferred_element_type=jnp.float32)
    spec_ref[...] = spec
    square = spec * spec
    square = square + swapped(square)
    peak = jnp.concatenate(
        [jnp.max(square[64 * kk : 64 * kk + 64], axis=0, keepdims=True) for kk in range(8)], 0
    )
    for shift in (1, 2, 4, 8, 16, 32):
        peak = jnp.maximum(peak, pltpu.roll(peak, shift, 1))
    limit = level_ref[...] * (jnp.sqrt(peak) + 1e-6)
    limit_ref[...] = jnp.broadcast_to(limit[None], limit_ref.shape)


def backward_kernel(spec_ref, limit_ref, place_ref, turn_ref, block_ref, out_ref, tmp):
    limit = jnp.max(limit_ref[...], axis=0)
    shrunk = []
    for kk in range(8):
        value = spec_ref[64 * kk : 64 * kk + 64, :]
        square = value * value
        size = jnp.sqrt(square + swapped(square))
        bound = limit[kk : kk + 1]
        factor = jnp.maximum(size - bound, 0.0) / jnp.maximum(size, bound)
        shrunk.append((value * factor).astype(jnp.bfloat16))
    product = jnp.dot(jnp.concatenate(shrunk, 0), block_ref[...], preferred_element_type=jnp.float32)
    cos, sin = turn_ref[:, :128], turn_ref[:, 128:]
    turned = []
    for kk in range(8):
        value = product[64 * kk : 64 * kk + 64]
        turned.append((value * cos - swapped(value) * sin).astype(jnp.bfloat16))
    product = jnp.dot(place_ref[...], jnp.concatenate(turned, 1), preferred_element_type=jnp.float32)
    half = lane_ids(64) < 64
    for kk in range(8):
        columns = slice(128 * kk, 128 * kk + 128)
        other = swapped(product[64:, columns])
        tmp[pl.ds(kk, 64, stride=8), :] = product[:64, columns] - jnp.where(half, other, -other)
    out_ref[...] = tmp[...].astype(jnp.bfloat16)


def time_back_kernel(x_ref, table_ref, out_ref):
    x = x_ref[...].astype(jnp.float32).reshape(DEVS // 2, 2, 8, 128)
    halves = []
    for parity in range(2):
        turned = x[:, parity].reshape(256, 128).T.astype(jnp.bfloat16)
        left = jnp.concatenate([turned[:64], turned[64:]], 1)
        table = table_ref[512 * parity : 512 * parity + 512, :]
        halves.append(jnp.dot(left, table, preferred_element_type=jnp.float32))
    for half, value in enumerate((halves[0] + halves[1], halves[0] - halves[1])):
        for c in range(CHANS):
            out_ref[:, c, 512 * half : 512 * half + 512] = value[BLOCK * c : BLOCK * c + BLOCK]


def vmem(count):
    return [pl.BlockSpec(memory_space=pltpu.VMEM)] * count


def smem():
    return pl.BlockSpec(memory_space=pltpu.SMEM)


def call(kernel, outs, in_specs, scratch=(), cost=None):
    return pl.pallas_call(
        kernel,
        out_shape=outs,
        in_specs=in_specs,
        out_specs=vmem(len(outs)) if isinstance(outs, list) else vmem(1)[0],
        scratch_shapes=list(scratch),
        compiler_params=pltpu.CompilerParams(vmem_limit_bytes=8 * 1024 * 1024),
        cost_estimate=cost,
        interpret=INTERPRET,
    )


def local(blended, estimate, neighbour_sources, partner_lags, threshold_level):
    own_lags = jnp.pad(jnp.concatenate([partner_lags[:, slot] for slot in range(6)]), (0, 32))
    own_lags = jnp.broadcast_to(own_lags, (DEVS, 128))
    all_lags = lax.all_to_all(own_lags, "shot", 0, 0, tiled=True)
    res, part, level = call(
        residual_kernel,
        [
            jax.ShapeDtypeStruct((36 * CHANS * 8, 128), jnp.float32),
            jax.ShapeDtypeStruct((192 * 8, 128), jnp.float32),
            jax.ShapeDtypeStruct((8, 128), jnp.float32),
        ],
        [smem()] + vmem(3),
        [
            pltpu.VMEM((BLOCK, CHANS, SAMPLES), jnp.float32),
            pltpu.VMEM((20 * CHANS * STEP + 16, 128), jnp.float32),
            pltpu.SMEM((128,), jnp.int32),
            pltpu.SemaphoreType.DMA,
        ],
        pl.CostEstimate(flops=4_000_000, bytes_accessed=16_000_000, transcendentals=0),
    )(threshold_level, own_lags, blended, estimate)
    rows = call(
        blend_kernel,
        jax.ShapeDtypeStruct((512, 512), jnp.bfloat16),
        vmem(3),
        [
            pltpu.VMEM((44 * CHANS * STEP + 16, 128), jnp.float32),
            pltpu.VMEM((2048, 128), jnp.float32),
            pltpu.SMEM((6, 128), jnp.int32),
            pltpu.SemaphoreType.DMA((6,)),
        ],
    )(all_lags, res, part)
    send = call(
        time_kernel,
        jax.ShapeDtypeStruct((DEVS * 24, 128), jnp.bfloat16),
        vmem(2),
        [pltpu.VMEM((DEVS // 2, 2, 24, 128), jnp.float32)],
    )(rows, time_table())
    columns = lax.all_to_all(send.reshape(DEVS, 24, 128), "shot", 0, 0, tiled=True).reshape(DEVS * 24, 128)
    others = lax.axis_size("chan")
    spec, limit = call(
        forward_kernel,
        [jax.ShapeDtypeStruct((512, 128), jnp.float32), jax.ShapeDtypeStruct((others, 8, 128), jnp.float32)],
        vmem(5),
        [pltpu.VMEM((512, 128), jnp.float32)],
    )(level, columns, place_table(), twiddles(), block_table(-1))
    limits = lax.all_to_all(limit, "chan", 0, 0, tiled=True)
    back = call(
        backward_kernel,
        jax.ShapeDtypeStruct((512, 128), jnp.bfloat16),
        vmem(5),
        [pltpu.VMEM((512, 128), jnp.float32)],
    )(spec, limits, place_table(), twiddles(), block_table(1))
    arrived = lax.all_to_all(back.reshape(DEVS, 8, 128), "shot", 0, 0, tiled=True).reshape(512, 128)
    return call(
        time_back_kernel,
        jax.ShapeDtypeStruct((BLOCK, CHANS, SAMPLES), jnp.float32),
        vmem(2),
    )(arrived, time_back_table())


def solution(mesh):
    shots = P("shot", "chan", None)
    return jax.shard_map(
        local,
        mesh=mesh,
        in_specs=(shots, shots, P("shot", None), P("shot", None), P()),
        out_specs=shots,
        check_vma=False,
    )
```

```python
import jax
import jax.numpy as jnp
import numpy as np
from jax import lax
from jax.experimental import pallas as pl
from jax.experimental.pallas import tpu as pltpu
from jax.sharding import PartitionSpec as P

SHOTS, SAMPLES, FREQS = 1024, 1024, 512
DEVS, BLOCK, CHANS = 64, 16, 4
STEP = 24
INTERPRET = False


def half_phases(parity):
    k = 2 * np.arange(FREQS // 2)[:, None] + parity
    t = np.arange(SAMPLES // 2)[None, :]
    return k, 2 * np.pi * ((t * k) % SAMPLES) / SAMPLES


def time_table():
    parts = []
    for parity in range(2):
        _, phase = half_phases(parity)
        parts += [np.cos(phase) / 32, -np.sin(phase) / 32]
    return np.concatenate(parts, 0).astype(jnp.bfloat16)


def time_back_table():
    parts = []
    for parity in range(2):
        k, phase = half_phases(parity)
        weight = np.where(k == 0, 1.0, 2.0) / 32
        parts += [weight * np.cos(phase), -weight * np.sin(phase)]
    return np.concatenate(parts, 0).astype(jnp.bfloat16)


def place_table():
    phase = 2 * np.pi * (np.arange(64)[:, None] * np.arange(64)[None, :] % 64) / 64
    return np.concatenate([np.cos(phase), np.sin(phase)], 0).astype(jnp.bfloat16)


def twiddles():
    phase = 2 * np.pi * np.arange(64)[:, None] * np.arange(BLOCK)[None, :] / SHOTS
    cos, sin = np.tile(np.cos(phase), (1, 8)), np.tile(np.sin(phase), (1, 8))
    sin[:, 64:] *= -1
    return np.concatenate([cos, sin], 1).astype(np.float32)


def block_table(sign):
    out = np.zeros((2, CHANS, 16, 2, CHANS, 16), np.float64)
    phase = 2 * np.pi * (np.arange(16)[:, None] * np.arange(16)[None, :] % 16) / 16
    for c in range(CHANS):
        out[0, c, :, 0, c, :] = np.cos(phase)
        out[1, c, :, 1, c, :] = np.cos(phase)
        out[0, c, :, 1, c, :] = sign * np.sin(phase)
        out[1, c, :, 0, c, :] = -sign * np.sin(phase)
    return (out.reshape(128, 128) / 32).astype(jnp.bfloat16)


def lane_ids(*shape):
    return lax.broadcasted_iota(jnp.int32, (*shape, 128), len(shape))


def swapped(value):
    return pltpu.roll(value, 64, value.ndim - 1)


def base(row, c):
    return (row * CHANS + c) * STEP + 16


def res_row(side, n):
    return side * 22 + n + 3


def place_of(side, n):
    low = 128 + (14 if side == 0 else 12) + n + 2
    high = 128 + (0 if side == 0 else 2) + n - 16
    return jnp.where(n < 0, low, jnp.where(n > 15, high, side * 64 + n))


def add_shifted(total, ref, first, lag, lanes):
    turn = lag & 127
    keep = lanes < 128 - turn
    first = first - (lag >> 7)
    for c in range(CHANS):
        here = ref[pl.ds(first + c * STEP, 8), :]
        before = ref[pl.ds(first + c * STEP - 1, 8), :]
        moved = pltpu.roll(jnp.where(keep, here, before), turn, 1)
        total[c] = moved if total[c] is None else total[c] + moved


def fleet_of(shot):
    return ((shot + 1) >> 9) & 1


def residual_kernel(level_ref, all_lags, dat_ref, est_ref, res, part, level_out, est, lag_ref, sem):
    copy = pltpu.make_async_copy(all_lags.at[0], lag_ref, sem)
    copy.start()
    place = lax.axis_index("shot")
    level_out[...] = jnp.full((8, 128), level_ref[0].astype(jnp.float32) * (1 / 64))
    est[...] = jnp.zeros_like(est)
    res[...] = jnp.zeros_like(res)
    part[1024:, :] = jnp.zeros((512, 128), jnp.float32)
    for c in range(CHANS):
        for u in range(8):
            columns = slice(128 * u, 128 * u + 128)
            est[pl.ds(base(2, c) + u, BLOCK, stride=CHANS * STEP), :] = est_ref[:, c, columns]
            res[pl.ds((CHANS + c) * 8 + u, BLOCK, stride=CHANS * 8), :] = dat_ref[:, c, columns]
    lanes = lane_ids(8)
    copy.wait()

    @pl.loop(0, BLOCK + 2, unroll=3)
    def _(step):
        n = step - 1
        for side in range(2):
            total = [None] * CHANS
            for ahead in (-1, 1) if side == 0 else (-1, 0, 1):
                m = jnp.clip(n + ahead, 0, BLOCK - 1)
                fleet = fleet_of(BLOCK * place + m)
                lag = -lag_ref[(3 * (fleet ^ side) + 1 - ahead) * BLOCK + m]
                add_shifted(total, est, base(n + ahead + 2, 0), lag, lanes)
            for c in range(CHANS):
                rows = pl.ds(((side * 18 + step) * CHANS + c) * 8, 8)
                value = -total[c] if side else res[rows, :] - total[c]
                res[rows, :] = value
                value = 0.25 * value
                if side == 0:
                    value = value + est[pl.ds(base(n + 2, c), 8), :]
                part[pl.ds((place_of(side, n) + c * BLOCK) * 8, 8), :] = value


def blend_kernel(all_lags, res_ref, part, out_ref, res, upd, lag_ref, sems):
    place = lax.axis_index("shot")
    copies = []
    for number in range(6):
        source = (place + number % 3 - 1 + 32 * (number // 3) + DEVS) & (DEVS - 1)
        copies.append(pltpu.make_async_copy(all_lags.at[source], lag_ref.at[number], sems.at[number]))
        copies[-1].start()
    upd[1024:, :] = jnp.zeros((1024, 128), jnp.float32)
    res[...] = jnp.zeros_like(res)
    for side in range(2):
        for row in range(18):
            for c in range(CHANS):
                at = ((side * 18 + row) * CHANS + c) * 8
                res[pl.ds(base(res_row(side, row - 1), c), 8), :] = res_ref[at : at + 8, :]
    lanes = lane_ids(8)
    for copy in copies:
        copy.wait()

    @pl.loop(0, BLOCK + 4, unroll=5)
    def _(step):
        n = step - 2
        for side in range(2):
            shot = (512 * side + BLOCK * place + n + SHOTS) & (SHOTS - 1)
            fleet = fleet_of(shot)
            total = [None] * CHANS
            for flip, ahead in ((0, -1), (0, 1), (1, -1), (1, 0), (1, 1)):
                lag = lag_ref[side * 3 + ((n + BLOCK) >> 4), (3 * (fleet ^ flip) + 1 + ahead) * BLOCK + (shot & 15)]
                add_shifted(total, res, base(res_row(side ^ flip, n + ahead), 0), lag, lanes)
            for c in range(CHANS):
                rows = pl.ds((place_of(side, n) + c * BLOCK) * 8, 8)
                upd[rows, :] = part[rows, :] + 0.25 * total[c]

    octaves = [upd[pl.ds(u, 256, stride=8), :] for u in range(8)]
    for parity in range(2):
        rows = [octaves[u] - octaves[u + 4] if parity else octaves[u] + octaves[u + 4] for u in range(4)]
        out_ref[256 * parity : 256 * parity + 256, :] = jnp.concatenate(rows, 1).astype(jnp.bfloat16)


def time_kernel(rows_ref, table, out_ref, acc):
    for parity in range(2):
        product = lax.dot_general(
            table[512 * parity : 512 * parity + 512, :],
            rows_ref[256 * parity : 256 * parity + 256, :],
            (((1,), (1,)), ((), ())),
            preferred_element_type=jnp.float32,
        )
        real, imag = product[:256], product[256:]
        for at, value in ((0, real[:, :128]), (8, imag[:, :128]), (16, real[:, 128:] + swapped(imag[:, 128:]))):
            acc[:, parity, at : at + 8, :] = value.reshape(DEVS // 2, 8, 128)
    out_ref[...] = acc[...].reshape(DEVS * 24, 128).astype(jnp.bfloat16)


def forward_kernel(level_ref, x_ref, place_ref, turn_ref, block_ref, spec_ref, limit_ref, tmp):
    x = x_ref[...].astype(jnp.float32).reshape(DEVS, 24, 128)
    real, imag, rims = x[:, :8], x[:, 8:16], x[:, 16:]

    def ahead(value, count):
        return jnp.concatenate([value[count:], value[:count]], 0)

    def lane_roll(value, shift):
        return pltpu.roll(value.reshape(512, 128), shift, 1).reshape(DEVS, 8, 128)

    lanes = lane_ids(DEVS, 8)
    within = lanes & 15
    total = jnp.where(
        lanes < 64,
        real + lane_roll(ahead(real, 32), 64),
        lane_roll(imag, 64) + ahead(imag, 32),
    )
    far = ahead(rims, 32)
    rims = rims + jnp.where(within < 8, lane_roll(far, 126), lane_roll(far, 2))
    total = total + jnp.where(within < 2, ahead(rims, 63), jnp.where(within >= 14, ahead(rims, 1), 0.0))
    tmp[...] = total.reshape(512, 128)
    rhs = jnp.concatenate([tmp[pl.ds(kk, 64, stride=8), :] for kk in range(8)], 1).astype(jnp.bfloat16)
    product = jnp.dot(place_ref[...], rhs, preferred_element_type=jnp.float32)
    cos, sin = turn_ref[:, :128], turn_ref[:, 128:]
    half = lane_ids(64) < 64
    turned = []
    for kk in range(8):
        columns = slice(128 * kk, 128 * kk + 128)
        other = swapped(product[64:, columns])
        value = product[:64, columns] + jnp.where(half, other, -other)
        turned.append((value * cos + swapped(value) * sin).astype(jnp.bfloat16))
    spec = jnp.dot(jnp.concatenate(turned, 0), block_ref[...], preferred_element_type=jnp.float32)
    spec_ref[...] = spec
    square = spec * spec
    square = square + swapped(square)
    peak = jnp.concatenate(
        [jnp.max(square[64 * kk : 64 * kk + 64], axis=0, keepdims=True) for kk in range(8)], 0
    )
    for shift in (1, 2, 4, 8, 16, 32):
        peak = jnp.maximum(peak, pltpu.roll(peak, shift, 1))
    limit = level_ref[...] * (jnp.sqrt(peak) + 1e-6)
    own = lane_ids(8) == lax.broadcasted_iota(jnp.int32, (8, 128), 0)
    limit_ref[...] = jnp.broadcast_to(jnp.sum(jnp.where(own, limit, 0.0), axis=0, keepdims=True), limit_ref.shape)


def backward_kernel(spec_ref, limit_ref, place_ref, turn_ref, block_ref, out_ref, tmp):
    limit = jnp.max(limit_ref[...], axis=0, keepdims=True)
    shrunk = []
    for kk in range(8):
        value = spec_ref[64 * kk : 64 * kk + 64, :]
        square = value * value
        size = jnp.sqrt(square + swapped(square))
        bound = limit[:, kk : kk + 1]
        factor = jnp.maximum(size - bound, 0.0) / jnp.maximum(size, bound)
        shrunk.append((value * factor).astype(jnp.bfloat16))
    product = jnp.dot(jnp.concatenate(shrunk, 0), block_ref[...], preferred_element_type=jnp.float32)
    cos, sin = turn_ref[:, :128], turn_ref[:, 128:]
    turned = []
    for kk in range(8):
        value = product[64 * kk : 64 * kk + 64]
        turned.append((value * cos - swapped(value) * sin).astype(jnp.bfloat16))
    product = jnp.dot(place_ref[...], jnp.concatenate(turned, 1), preferred_element_type=jnp.float32)
    half = lane_ids(64) < 64
    for kk in range(8):
        columns = slice(128 * kk, 128 * kk + 128)
        other = swapped(product[64:, columns])
        tmp[pl.ds(kk, 64, stride=8), :] = product[:64, columns] - jnp.where(half, other, -other)
    out_ref[...] = tmp[...].astype(jnp.bfloat16)


def time_back_kernel(x_ref, table_ref, out_ref):
    x = x_ref[...].astype(jnp.float32).reshape(DEVS // 2, 2, 8, 128)
    halves = []
    for parity in range(2):
        turned = x[:, parity].reshape(256, 128).T.astype(jnp.bfloat16)
        left = jnp.concatenate([turned[:64], turned[64:]], 1)
        table = table_ref[512 * parity : 512 * parity + 512, :]
        halves.append(jnp.dot(left, table, preferred_element_type=jnp.float32))
    for half, value in enumerate((halves[0] + halves[1], halves[0] - halves[1])):
        for c in range(CHANS):
            out_ref[:, c, 512 * half : 512 * half + 512] = value[BLOCK * c : BLOCK * c + BLOCK]


def vmem(count):
    return [pl.BlockSpec(memory_space=pltpu.VMEM)] * count


def smem():
    return pl.BlockSpec(memory_space=pltpu.SMEM)


def call(kernel, outs, in_specs, scratch=(), cost=None):
    return pl.pallas_call(
        kernel,
        out_shape=outs,
        in_specs=in_specs,
        out_specs=vmem(len(outs)) if isinstance(outs, list) else vmem(1)[0],
        scratch_shapes=list(scratch),
        compiler_params=pltpu.CompilerParams(vmem_limit_bytes=8 * 1024 * 1024),
        cost_estimate=cost,
        interpret=INTERPRET,
    )


def local(blended, estimate, neighbour_sources, partner_lags, threshold_level):
    own_lags = jnp.pad(jnp.concatenate([partner_lags[:, slot] for slot in range(6)]), (0, 32))
    own_lags = jnp.broadcast_to(own_lags, (DEVS, 128))
    all_lags = lax.all_to_all(own_lags, "shot", 0, 0, tiled=True)
    old = estimate.astype(jnp.float32)
    res, part, level = call(
        residual_kernel,
        [
            jax.ShapeDtypeStruct((36 * CHANS * 8, 128), jnp.float32),
            jax.ShapeDtypeStruct((192 * 8, 128), jnp.float32),
            jax.ShapeDtypeStruct((8, 128), jnp.float32),
        ],
        [smem()] + vmem(3),
        [
            pltpu.VMEM((20 * CHANS * STEP + 16, 128), jnp.float32),
            pltpu.SMEM((128,), jnp.int32),
            pltpu.SemaphoreType.DMA,
        ],
        pl.CostEstimate(flops=4_000_000, bytes_accessed=16_000_000, transcendentals=0),
    )(threshold_level, own_lags, blended - old, old)
    rows = call(
        blend_kernel,
        jax.ShapeDtypeStruct((512, 512), jnp.bfloat16),
        vmem(3),
        [
            pltpu.VMEM((44 * CHANS * STEP + 16, 128), jnp.float32),
            pltpu.VMEM((2048, 128), jnp.float32),
            pltpu.SMEM((6, 128), jnp.int32),
            pltpu.SemaphoreType.DMA((6,)),
        ],
    )(all_lags, res, part)
    send = call(
        time_kernel,
        jax.ShapeDtypeStruct((DEVS * 24, 128), jnp.bfloat16),
        vmem(2),
        [pltpu.VMEM((DEVS // 2, 2, 24, 128), jnp.float32)],
    )(rows, time_table())
    columns = lax.all_to_all(send.reshape(DEVS, 24, 128), "shot", 0, 0, tiled=True).reshape(DEVS * 24, 128)
    others = lax.axis_size("chan")
    spec, limit = call(
        forward_kernel,
        [jax.ShapeDtypeStruct((512, 128), jnp.float32), jax.ShapeDtypeStruct((others, 128), jnp.float32)],
        vmem(5),
        [pltpu.VMEM((512, 128), jnp.float32)],
    )(level, columns, place_table(), twiddles(), block_table(-1))
    limits = lax.all_to_all(limit, "chan", 0, 0, tiled=True)
    back = call(
        backward_kernel,
        jax.ShapeDtypeStruct((512, 128), jnp.bfloat16),
        vmem(5),
        [pltpu.VMEM((512, 128), jnp.float32)],
    )(spec, limits, place_table(), twiddles(), block_table(1))
    arrived = lax.all_to_all(back.reshape(DEVS, 8, 128), "shot", 0, 0, tiled=True).reshape(512, 128)
    return call(
        time_back_kernel,
        jax.ShapeDtypeStruct((BLOCK, CHANS, SAMPLES), jnp.float32),
        vmem(2),
    )(arrived, time_back_table())


def solution(mesh):
    shots = P("shot", "chan", None)
    return jax.shard_map(
        local,
        mesh=mesh,
        in_specs=(shots, shots, P("shot", None), P("shot", None), P()),
        out_specs=shots,
        check_vma=False,
    )
```

```python
import jax
import jax.numpy as jnp
import numpy as np
from jax import lax
from jax.experimental import pallas as pl
from jax.experimental.pallas import tpu as pltpu
from jax.sharding import PartitionSpec as P

SHOTS, SAMPLES, FREQS = 1024, 1024, 512
DEVS, BLOCK, CHANS = 64, 16, 4
STEP = 24
INTERPRET = False


def half_phases(parity):
    k = 2 * np.arange(FREQS // 2)[:, None] + parity
    t = np.arange(SAMPLES // 2)[None, :]
    return k, 2 * np.pi * ((t * k) % SAMPLES) / SAMPLES


def time_table():
    parts = []
    for parity in range(2):
        _, phase = half_phases(parity)
        parts += [np.cos(phase) / 32, -np.sin(phase) / 32]
    return np.concatenate(parts, 0).astype(jnp.bfloat16)


def time_back_table():
    parts = []
    for parity in range(2):
        k, phase = half_phases(parity)
        weight = np.where(k == 0, 1.0, 2.0) / 32
        parts += [weight * np.cos(phase), -weight * np.sin(phase)]
    return np.concatenate(parts, 0).astype(jnp.bfloat16)


def place_table():
    phase = 2 * np.pi * (np.arange(64)[:, None] * np.arange(64)[None, :] % 64) / 64
    return np.concatenate([np.cos(phase), np.sin(phase)], 0).astype(jnp.bfloat16)


def twiddles():
    phase = 2 * np.pi * np.arange(64)[:, None] * np.arange(BLOCK)[None, :] / SHOTS
    cos, sin = np.tile(np.cos(phase), (1, 8)), np.tile(np.sin(phase), (1, 8))
    sin[:, 64:] *= -1
    return np.concatenate([cos, sin], 1).astype(np.float32)


def block_table(sign):
    out = np.zeros((2, CHANS, 16, 2, CHANS, 16), np.float64)
    phase = 2 * np.pi * (np.arange(16)[:, None] * np.arange(16)[None, :] % 16) / 16
    for c in range(CHANS):
        out[0, c, :, 0, c, :] = np.cos(phase)
        out[1, c, :, 1, c, :] = np.cos(phase)
        out[0, c, :, 1, c, :] = sign * np.sin(phase)
        out[1, c, :, 0, c, :] = -sign * np.sin(phase)
    return (out.reshape(128, 128) / 32).astype(jnp.bfloat16)


def lane_ids(*shape):
    return lax.broadcasted_iota(jnp.int32, (*shape, 128), len(shape))


def swapped(value):
    return pltpu.roll(value, 64, value.ndim - 1)


def base(row, c):
    return (row * CHANS + c) * STEP + 16


def res_row(side, n):
    return side * 22 + n + 3


def place_of(side, n):
    low = 128 + (14 if side == 0 else 12) + n + 2
    high = 128 + (0 if side == 0 else 2) + n - 16
    return jnp.where(n < 0, low, jnp.where(n > 15, high, side * 64 + n))


def add_shifted(total, ref, first, lag, lanes):
    turn = lag & 127
    keep = lanes < 128 - turn
    first = first - (lag >> 7)
    for c in range(CHANS):
        here = ref[pl.ds(first + c * STEP, 8), :]
        before = ref[pl.ds(first + c * STEP - 1, 8), :]
        moved = pltpu.roll(jnp.where(keep, here, before), turn, 1)
        total[c] = moved if total[c] is None else total[c] + moved


def fleet_of(shot):
    return ((shot + 1) >> 9) & 1


def residual_kernel(level_ref, all_lags, dat_ref, est_ref, res, part, level_out, est, lag_ref, sem):
    copy = pltpu.make_async_copy(all_lags.at[0], lag_ref, sem)
    copy.start()
    place = lax.axis_index("shot")
    level_out[...] = jnp.full((8, 128), level_ref[0].astype(jnp.float32) * (1 / 64))
    est[...] = jnp.zeros_like(est)
    res[...] = jnp.zeros_like(res)
    part[1024:, :] = jnp.zeros((512, 128), jnp.float32)
    for c in range(CHANS):
        for u in range(8):
            columns = slice(128 * u, 128 * u + 128)
            est[pl.ds(base(2, c) + u, BLOCK, stride=CHANS * STEP), :] = est_ref[:, c, columns]
            res[pl.ds((CHANS + c) * 8 + u, BLOCK, stride=CHANS * 8), :] = dat_ref[:, c, columns]
    lanes = lane_ids(8)
    copy.wait()

    @pl.loop(0, BLOCK + 2, unroll=3)
    def _(step):
        n = step - 1
        for side in range(2):
            total = [None] * CHANS
            for ahead in (-1, 1) if side == 0 else (-1, 0, 1):
                m = jnp.clip(n + ahead, 0, BLOCK - 1)
                fleet = fleet_of(BLOCK * place + m)
                lag = -lag_ref[(3 * (fleet ^ side) + 1 - ahead) * BLOCK + m]
                add_shifted(total, est, base(n + ahead + 2, 0), lag, lanes)
            for c in range(CHANS):
                rows = pl.ds(((side * 18 + step) * CHANS + c) * 8, 8)
                value = -total[c] if side else res[rows, :] - total[c]
                res[rows, :] = value
                value = 0.25 * value
                if side == 0:
                    value = value + est[pl.ds(base(n + 2, c), 8), :]
                part[pl.ds((place_of(side, n) + c * BLOCK) * 8, 8), :] = value


def blend_kernel(all_lags, res_ref, part, out_ref, res, upd, lag_ref, sems):
    place = lax.axis_index("shot")
    copies = []
    for number in range(6):
        source = (place + number % 3 - 1 + 32 * (number // 3) + DEVS) & (DEVS - 1)
        copies.append(pltpu.make_async_copy(all_lags.at[source], lag_ref.at[number], sems.at[number]))
        copies[-1].start()
    upd[1024:, :] = jnp.zeros((1024, 128), jnp.float32)
    res[...] = jnp.zeros_like(res)
    for side in range(2):
        for row in range(18):
            for c in range(CHANS):
                at = ((side * 18 + row) * CHANS + c) * 8
                res[pl.ds(base(res_row(side, row - 1), c), 8), :] = res_ref[at : at + 8, :]
    lanes = lane_ids(8)
    for copy in copies:
        copy.wait()

    def add_row(n, steps):
        for side in range(2):
            shot = (512 * side + BLOCK * place + n + SHOTS) & (SHOTS - 1)
            fleet = fleet_of(shot)
            total = [None] * CHANS
            for flip, ahead in ((0, -1), (0, 1), (1, -1), (1, 0), (1, 1)):
                if ahead not in steps:
                    continue
                lag = lag_ref[side * 3 + ((n + BLOCK) >> 4), (3 * (fleet ^ flip) + 1 + ahead) * BLOCK + (shot & 15)]
                add_shifted(total, res, base(res_row(side ^ flip, n + ahead), 0), lag, lanes)
            for c in range(CHANS):
                rows = pl.ds((place_of(side, n) + c * BLOCK) * 8, 8)
                upd[rows, :] = part[rows, :] + 0.25 * total[c]

    for n, steps in ((-2, (1,)), (-1, (0, 1)), (BLOCK, (-1, 0)), (BLOCK + 1, (-1,))):
        add_row(n, steps)

    @pl.loop(0, BLOCK, unroll=4)
    def _(n):
        add_row(n, (-1, 0, 1))

    octaves = [upd[pl.ds(u, 256, stride=8), :] for u in range(8)]
    for parity in range(2):
        rows = [octaves[u] - octaves[u + 4] if parity else octaves[u] + octaves[u + 4] for u in range(4)]
        out_ref[256 * parity : 256 * parity + 256, :] = jnp.concatenate(rows, 1).astype(jnp.bfloat16)


def time_kernel(rows_ref, table, out_ref, acc):
    for parity in range(2):
        product = lax.dot_general(
            table[512 * parity : 512 * parity + 512, :],
            rows_ref[256 * parity : 256 * parity + 256, :],
            (((1,), (1,)), ((), ())),
            preferred_element_type=jnp.float32,
        )
        real, imag = product[:256], product[256:]
        for at, value in ((0, real[:, :128]), (8, imag[:, :128]), (16, real[:, 128:] + swapped(imag[:, 128:]))):
            acc[:, parity, at : at + 8, :] = value.reshape(DEVS // 2, 8, 128)
    out_ref[...] = acc[...].reshape(DEVS * 24, 128).astype(jnp.bfloat16)


def forward_kernel(level_ref, x_ref, place_ref, turn_ref, block_ref, spec_ref, limit_ref, tmp):
    x = x_ref[...].astype(jnp.float32).reshape(DEVS, 24, 128)
    real, imag, rims = x[:, :8], x[:, 8:16], x[:, 16:]

    def ahead(value, count):
        return jnp.concatenate([value[count:], value[:count]], 0)

    def lane_roll(value, shift):
        return pltpu.roll(value.reshape(512, 128), shift, 1).reshape(DEVS, 8, 128)

    lanes = lane_ids(DEVS, 8)
    within = lanes & 15
    total = jnp.where(
        lanes < 64,
        real + lane_roll(ahead(real, 32), 64),
        lane_roll(imag, 64) + ahead(imag, 32),
    )
    far = ahead(rims, 32)
    rims = rims + jnp.where(within < 8, lane_roll(far, 126), lane_roll(far, 2))
    total = total + jnp.where(within < 2, ahead(rims, 63), jnp.where(within >= 14, ahead(rims, 1), 0.0))
    tmp[...] = total.reshape(512, 128)
    rhs = jnp.concatenate([tmp[pl.ds(kk, 64, stride=8), :] for kk in range(8)], 1).astype(jnp.bfloat16)
    product = jnp.dot(place_ref[...], rhs, preferred_element_type=jnp.float32)
    cos, sin = turn_ref[:, :128], turn_ref[:, 128:]
    half = lane_ids(64) < 64
    turned = []
    for kk in range(8):
        columns = slice(128 * kk, 128 * kk + 128)
        other = swapped(product[64:, columns])
        value = product[:64, columns] + jnp.where(half, other, -other)
        turned.append((value * cos + swapped(value) * sin).astype(jnp.bfloat16))
    spec = jnp.dot(jnp.concatenate(turned, 0), block_ref[...], preferred_element_type=jnp.float32)
    spec_ref[...] = spec
    square = spec * spec
    square = square + swapped(square)
    peak = jnp.concatenate(
        [jnp.max(square[64 * kk : 64 * kk + 64], axis=0, keepdims=True) for kk in range(8)], 0
    )
    for shift in (1, 2, 4, 8, 16, 32):
        peak = jnp.maximum(peak, pltpu.roll(peak, shift, 1))
    limit = level_ref[...] * (jnp.sqrt(peak) + 1e-6)
    own = lane_ids(8) == lax.broadcasted_iota(jnp.int32, (8, 128), 0)
    limit_ref[...] = jnp.broadcast_to(jnp.sum(jnp.where(own, limit, 0.0), axis=0, keepdims=True), limit_ref.shape)


def backward_kernel(spec_ref, limit_ref, place_ref, turn_ref, block_ref, out_ref, tmp):
    limit = jnp.max(limit_ref[...], axis=0, keepdims=True)
    shrunk = []
    for kk in range(8):
        value = spec_ref[64 * kk : 64 * kk + 64, :]
        square = value * value
        size = jnp.sqrt(square + swapped(square))
        bound = limit[:, kk : kk + 1]
        factor = jnp.maximum(size - bound, 0.0) / jnp.maximum(size, bound)
        shrunk.append((value * factor).astype(jnp.bfloat16))
    product = jnp.dot(jnp.concatenate(shrunk, 0), block_ref[...], preferred_element_type=jnp.float32)
    cos, sin = turn_ref[:, :128], turn_ref[:, 128:]
    turned = []
    for kk in range(8):
        value = product[64 * kk : 64 * kk + 64]
        turned.append((value * cos - swapped(value) * sin).astype(jnp.bfloat16))
    product = jnp.dot(place_ref[...], jnp.concatenate(turned, 1), preferred_element_type=jnp.float32)
    half = lane_ids(64) < 64
    for kk in range(8):
        columns = slice(128 * kk, 128 * kk + 128)
        other = swapped(product[64:, columns])
        tmp[pl.ds(kk, 64, stride=8), :] = product[:64, columns] - jnp.where(half, other, -other)
    out_ref[...] = tmp[...].astype(jnp.bfloat16)


def time_back_kernel(x_ref, table_ref, out_ref):
    x = x_ref[...].astype(jnp.float32).reshape(DEVS // 2, 2, 8, 128)
    halves = []
    for parity in range(2):
        turned = x[:, parity].reshape(256, 128).T.astype(jnp.bfloat16)
        left = jnp.concatenate([turned[:64], turned[64:]], 1)
        table = table_ref[512 * parity : 512 * parity + 512, :]
        halves.append(jnp.dot(left, table, preferred_element_type=jnp.float32))
    for half, value in enumerate((halves[0] + halves[1], halves[0] - halves[1])):
        for c in range(CHANS):
            out_ref[:, c, 512 * half : 512 * half + 512] = value[BLOCK * c : BLOCK * c + BLOCK]


def vmem(count):
    return [pl.BlockSpec(memory_space=pltpu.VMEM)] * count


def smem():
    return pl.BlockSpec(memory_space=pltpu.SMEM)


def call(kernel, outs, in_specs, scratch=(), cost=None):
    return pl.pallas_call(
        kernel,
        out_shape=outs,
        in_specs=in_specs,
        out_specs=vmem(len(outs)) if isinstance(outs, list) else vmem(1)[0],
        scratch_shapes=list(scratch),
        compiler_params=pltpu.CompilerParams(vmem_limit_bytes=8 * 1024 * 1024),
        cost_estimate=cost,
        interpret=INTERPRET,
    )


def local(blended, estimate, neighbour_sources, partner_lags, threshold_level):
    own_lags = jnp.pad(jnp.concatenate([partner_lags[:, slot] for slot in range(6)]), (0, 32))
    own_lags = jnp.broadcast_to(own_lags, (DEVS, 128))
    all_lags = lax.all_to_all(own_lags, "shot", 0, 0, tiled=True)
    old = estimate.astype(jnp.float32)
    res, part, level = call(
        residual_kernel,
        [
            jax.ShapeDtypeStruct((36 * CHANS * 8, 128), jnp.float32),
            jax.ShapeDtypeStruct((192 * 8, 128), jnp.float32),
            jax.ShapeDtypeStruct((8, 128), jnp.float32),
        ],
        [smem()] + vmem(3),
        [
            pltpu.VMEM((20 * CHANS * STEP + 16, 128), jnp.float32),
            pltpu.SMEM((128,), jnp.int32),
            pltpu.SemaphoreType.DMA,
        ],
        pl.CostEstimate(flops=4_000_000, bytes_accessed=16_000_000, transcendentals=0),
    )(threshold_level, own_lags, blended - old, old)
    rows = call(
        blend_kernel,
        jax.ShapeDtypeStruct((512, 512), jnp.bfloat16),
        vmem(3),
        [
            pltpu.VMEM((44 * CHANS * STEP + 16, 128), jnp.float32),
            pltpu.VMEM((2048, 128), jnp.float32),
            pltpu.SMEM((6, 128), jnp.int32),
            pltpu.SemaphoreType.DMA((6,)),
        ],
    )(all_lags, res, part)
    send = call(
        time_kernel,
        jax.ShapeDtypeStruct((DEVS * 24, 128), jnp.bfloat16),
        vmem(2),
        [pltpu.VMEM((DEVS // 2, 2, 24, 128), jnp.float32)],
    )(rows, time_table())
    columns = lax.all_to_all(send.reshape(DEVS, 24, 128), "shot", 0, 0, tiled=True).reshape(DEVS * 24, 128)
    others = lax.axis_size("chan")
    spec, limit = call(
        forward_kernel,
        [jax.ShapeDtypeStruct((512, 128), jnp.float32), jax.ShapeDtypeStruct((others, 128), jnp.float32)],
        vmem(5),
        [pltpu.VMEM((512, 128), jnp.float32)],
    )(level, columns, place_table(), twiddles(), block_table(-1))
    limits = lax.all_to_all(limit, "chan", 0, 0, tiled=True)
    back = call(
        backward_kernel,
        jax.ShapeDtypeStruct((512, 128), jnp.bfloat16),
        vmem(5),
        [pltpu.VMEM((512, 128), jnp.float32)],
    )(spec, limits, place_table(), twiddles(), block_table(1))
    arrived = lax.all_to_all(back.reshape(DEVS, 8, 128), "shot", 0, 0, tiled=True).reshape(512, 128)
    return call(
        time_back_kernel,
        jax.ShapeDtypeStruct((BLOCK, CHANS, SAMPLES), jnp.float32),
        vmem(2),
    )(arrived, time_back_table())


def solution(mesh):
    shots = P("shot", "chan", None)
    return jax.shard_map(
        local,
        mesh=mesh,
        in_specs=(shots, shots, P("shot", None), P("shot", None), P()),
        out_specs=shots,
        check_vma=False,
    )
```

```python
import jax
import jax.numpy as jnp
import numpy as np
from jax import lax
from jax.experimental import pallas as pl
from jax.experimental.pallas import tpu as pltpu
from jax.sharding import PartitionSpec as P

SHOTS, SAMPLES, FREQS = 1024, 1024, 512
DEVS, BLOCK, CHANS = 64, 16, 4
STEP = 24
INTERPRET = False


def half_phases(parity):
    k = 2 * np.arange(FREQS // 2)[:, None] + parity
    t = np.arange(SAMPLES // 2)[None, :]
    return k, 2 * np.pi * ((t * k) % SAMPLES) / SAMPLES


def time_table():
    parts = []
    for parity in range(2):
        _, phase = half_phases(parity)
        parts += [np.cos(phase) / 32, -np.sin(phase) / 32]
    return np.concatenate(parts, 0).astype(jnp.bfloat16)


def time_back_table():
    parts = []
    for parity in range(2):
        k, phase = half_phases(parity)
        weight = np.where(k == 0, 1.0, 2.0) / 32
        parts += [weight * np.cos(phase), -weight * np.sin(phase)]
    return np.concatenate(parts, 0).astype(jnp.bfloat16)


def place_table():
    phase = 2 * np.pi * (np.arange(64)[:, None] * np.arange(64)[None, :] % 64) / 64
    return np.concatenate([np.cos(phase), np.sin(phase)], 0).astype(jnp.bfloat16)


def twiddles():
    phase = 2 * np.pi * np.arange(64)[:, None] * np.arange(BLOCK)[None, :] / SHOTS
    cos, sin = np.tile(np.cos(phase), (1, 8)), np.tile(np.sin(phase), (1, 8))
    sin[:, 64:] *= -1
    return np.concatenate([cos, sin], 1).astype(np.float32)


def block_table(sign):
    out = np.zeros((2, CHANS, 16, 2, CHANS, 16), np.float64)
    phase = 2 * np.pi * (np.arange(16)[:, None] * np.arange(16)[None, :] % 16) / 16
    for c in range(CHANS):
        out[0, c, :, 0, c, :] = np.cos(phase)
        out[1, c, :, 1, c, :] = np.cos(phase)
        out[0, c, :, 1, c, :] = sign * np.sin(phase)
        out[1, c, :, 0, c, :] = -sign * np.sin(phase)
    return (out.reshape(128, 128) / 32).astype(jnp.bfloat16)


def lane_ids(*shape):
    return lax.broadcasted_iota(jnp.int32, (*shape, 128), len(shape))


def swapped(value):
    return pltpu.roll(value, 64, value.ndim - 1)


def base(row, c):
    return (row * CHANS + c) * STEP + 16


def res_row(side, n):
    return side * 22 + n + 3


def place_of(side, n):
    low = 128 + (14 if side == 0 else 12) + n + 2
    high = 128 + (0 if side == 0 else 2) + n - 16
    return jnp.where(n < 0, low, jnp.where(n > 15, high, side * 64 + n))


def add_shifted(total, ref, first, lag, lanes):
    turn = lag & 127
    keep = lanes < 128 - turn
    first = first - (lag >> 7)
    for c in range(CHANS):
        here = ref[pl.ds(first + c * STEP, 8), :]
        before = ref[pl.ds(first + c * STEP - 1, 8), :]
        moved = pltpu.roll(jnp.where(keep, here, before), turn, 1)
        total[c] = moved if total[c] is None else total[c] + moved


def fleet_of(shot):
    return ((shot + 1) >> 9) & 1


def residual_kernel(level_ref, all_lags, dat_ref, est_ref, res, part, level_out, est, lag_ref, sem):
    copy = pltpu.make_async_copy(all_lags.at[0], lag_ref, sem)
    copy.start()
    place = lax.axis_index("shot")
    level_out[...] = jnp.full((8, 128), level_ref[0].astype(jnp.float32) * (1 / 64))
    est[...] = jnp.zeros_like(est)
    res[...] = jnp.zeros_like(res)
    part[1024:, :] = jnp.zeros((512, 128), jnp.float32)
    for c in range(CHANS):
        for u in range(8):
            columns = slice(128 * u, 128 * u + 128)
            est[pl.ds(base(2, c) + u, BLOCK, stride=CHANS * STEP), :] = est_ref[:, c, columns]
            res[pl.ds((CHANS + c) * 8 + u, BLOCK, stride=CHANS * 8), :] = dat_ref[:, c, columns]
    lanes = lane_ids(8)
    copy.wait()

    @pl.loop(0, BLOCK + 2, unroll=6)
    def _(step):
        n = step - 1
        for side in range(2):
            total = [None] * CHANS
            for ahead in (-1, 1) if side == 0 else (-1, 0, 1):
                m = jnp.clip(n + ahead, 0, BLOCK - 1)
                fleet = fleet_of(BLOCK * place + m)
                lag = -lag_ref[(3 * (fleet ^ side) + 1 - ahead) * BLOCK + m]
                add_shifted(total, est, base(n + ahead + 2, 0), lag, lanes)
            for c in range(CHANS):
                rows = pl.ds(((side * 18 + step) * CHANS + c) * 8, 8)
                value = -total[c] if side else res[rows, :] - total[c]
                res[rows, :] = value
                value = 0.25 * value
                if side == 0:
                    value = value + est[pl.ds(base(n + 2, c), 8), :]
                part[pl.ds((place_of(side, n) + c * BLOCK) * 8, 8), :] = value


def blend_kernel(all_lags, res_ref, part, out_ref, res, upd, lag_ref, sems):
    place = lax.axis_index("shot")
    copies = []
    for number in range(6):
        source = (place + number % 3 - 1 + 32 * (number // 3) + DEVS) & (DEVS - 1)
        copies.append(pltpu.make_async_copy(all_lags.at[source], lag_ref.at[number], sems.at[number]))
        copies[-1].start()
    upd[1024:, :] = jnp.zeros((1024, 128), jnp.float32)
    res[...] = jnp.zeros_like(res)
    for side in range(2):
        for row in range(18):
            for c in range(CHANS):
                at = ((side * 18 + row) * CHANS + c) * 8
                res[pl.ds(base(res_row(side, row - 1), c), 8), :] = res_ref[at : at + 8, :]
    lanes = lane_ids(8)
    for copy in copies:
        copy.wait()

    @pl.loop(0, BLOCK + 4, unroll=10)
    def _(step):
        n = step - 2
        for side in range(2):
            shot = (512 * side + BLOCK * place + n + SHOTS) & (SHOTS - 1)
            fleet = fleet_of(shot)
            total = [None] * CHANS
            for flip, ahead in ((0, -1), (0, 1), (1, -1), (1, 0), (1, 1)):
                lag = lag_ref[side * 3 + ((n + BLOCK) >> 4), (3 * (fleet ^ flip) + 1 + ahead) * BLOCK + (shot & 15)]
                add_shifted(total, res, base(res_row(side ^ flip, n + ahead), 0), lag, lanes)
            for c in range(CHANS):
                rows = pl.ds((place_of(side, n) + c * BLOCK) * 8, 8)
                upd[rows, :] = part[rows, :] + 0.25 * total[c]

    octaves = [upd[pl.ds(u, 256, stride=8), :] for u in range(8)]
    for parity in range(2):
        rows = [octaves[u] - octaves[u + 4] if parity else octaves[u] + octaves[u + 4] for u in range(4)]
        out_ref[256 * parity : 256 * parity + 256, :] = jnp.concatenate(rows, 1).astype(jnp.bfloat16)


def time_kernel(rows_ref, table, out_ref, acc):
    for parity in range(2):
        product = lax.dot_general(
            table[512 * parity : 512 * parity + 512, :],
            rows_ref[256 * parity : 256 * parity + 256, :],
            (((1,), (1,)), ((), ())),
            preferred_element_type=jnp.float32,
        )
        real, imag = product[:256], product[256:]
        for at, value in ((0, real[:, :128]), (8, imag[:, :128]), (16, real[:, 128:] + swapped(imag[:, 128:]))):
            acc[:, parity, at : at + 8, :] = value.reshape(DEVS // 2, 8, 128)
    out_ref[...] = acc[...].reshape(DEVS * 24, 128).astype(jnp.bfloat16)


def forward_kernel(level_ref, x_ref, place_ref, turn_ref, block_ref, spec_ref, limit_ref, tmp):
    x = x_ref[...].astype(jnp.float32).reshape(DEVS, 24, 128)
    real, imag, rims = x[:, :8], x[:, 8:16], x[:, 16:]

    def ahead(value, count):
        return jnp.concatenate([value[count:], value[:count]], 0)

    def lane_roll(value, shift):
        return pltpu.roll(value.reshape(512, 128), shift, 1).reshape(DEVS, 8, 128)

    lanes = lane_ids(DEVS, 8)
    within = lanes & 15
    total = jnp.where(
        lanes < 64,
        real + lane_roll(ahead(real, 32), 64),
        lane_roll(imag, 64) + ahead(imag, 32),
    )
    far = ahead(rims, 32)
    rims = rims + jnp.where(within < 8, lane_roll(far, 126), lane_roll(far, 2))
    total = total + jnp.where(within < 2, ahead(rims, 63), jnp.where(within >= 14, ahead(rims, 1), 0.0))
    tmp[...] = total.reshape(512, 128)
    rhs = jnp.concatenate([tmp[pl.ds(kk, 64, stride=8), :] for kk in range(8)], 1).astype(jnp.bfloat16)
    product = jnp.dot(place_ref[...], rhs, preferred_element_type=jnp.float32)
    cos, sin = turn_ref[:, :128], turn_ref[:, 128:]
    half = lane_ids(64) < 64
    turned = []
    for kk in range(8):
        columns = slice(128 * kk, 128 * kk + 128)
        other = swapped(product[64:, columns])
        value = product[:64, columns] + jnp.where(half, other, -other)
        turned.append((value * cos + swapped(value) * sin).astype(jnp.bfloat16))
    spec = jnp.dot(jnp.concatenate(turned, 0), block_ref[...], preferred_element_type=jnp.float32)
    spec_ref[...] = spec
    square = spec * spec
    square = square + swapped(square)
    peak = jnp.concatenate(
        [jnp.max(square[64 * kk : 64 * kk + 64], axis=0, keepdims=True) for kk in range(8)], 0
    )
    for shift in (1, 2, 4, 8, 16, 32):
        peak = jnp.maximum(peak, pltpu.roll(peak, shift, 1))
    limit = level_ref[...] * (jnp.sqrt(peak) + 1e-6)
    own = lane_ids(8) == lax.broadcasted_iota(jnp.int32, (8, 128), 0)
    limit_ref[...] = jnp.broadcast_to(jnp.sum(jnp.where(own, limit, 0.0), axis=0, keepdims=True), limit_ref.shape)


def backward_kernel(spec_ref, limit_ref, place_ref, turn_ref, block_ref, out_ref, tmp):
    limit = jnp.max(limit_ref[...], axis=0, keepdims=True)
    shrunk = []
    for kk in range(8):
        value = spec_ref[64 * kk : 64 * kk + 64, :]
        square = value * value
        size = jnp.sqrt(square + swapped(square))
        bound = limit[:, kk : kk + 1]
        factor = jnp.maximum(size - bound, 0.0) / jnp.maximum(size, bound)
        shrunk.append((value * factor).astype(jnp.bfloat16))
    product = jnp.dot(jnp.concatenate(shrunk, 0), block_ref[...], preferred_element_type=jnp.float32)
    cos, sin = turn_ref[:, :128], turn_ref[:, 128:]
    turned = []
    for kk in range(8):
        value = product[64 * kk : 64 * kk + 64]
        turned.append((value * cos - swapped(value) * sin).astype(jnp.bfloat16))
    product = jnp.dot(place_ref[...], jnp.concatenate(turned, 1), preferred_element_type=jnp.float32)
    half = lane_ids(64) < 64
    for kk in range(8):
        columns = slice(128 * kk, 128 * kk + 128)
        other = swapped(product[64:, columns])
        tmp[pl.ds(kk, 64, stride=8), :] = product[:64, columns] - jnp.where(half, other, -other)
    out_ref[...] = tmp[...].astype(jnp.bfloat16)


def time_back_kernel(x_ref, table_ref, out_ref):
    x = x_ref[...].astype(jnp.float32).reshape(DEVS // 2, 2, 8, 128)
    halves = []
    for parity in range(2):
        turned = x[:, parity].reshape(256, 128).T.astype(jnp.bfloat16)
        left = jnp.concatenate([turned[:64], turned[64:]], 1)
        table = table_ref[512 * parity : 512 * parity + 512, :]
        halves.append(jnp.dot(left, table, preferred_element_type=jnp.float32))
    for half, value in enumerate((halves[0] + halves[1], halves[0] - halves[1])):
        for c in range(CHANS):
            out_ref[:, c, 512 * half : 512 * half + 512] = value[BLOCK * c : BLOCK * c + BLOCK]


def vmem(count):
    return [pl.BlockSpec(memory_space=pltpu.VMEM)] * count


def smem():
    return pl.BlockSpec(memory_space=pltpu.SMEM)


def call(kernel, outs, in_specs, scratch=(), cost=None):
    return pl.pallas_call(
        kernel,
        out_shape=outs,
        in_specs=in_specs,
        out_specs=vmem(len(outs)) if isinstance(outs, list) else vmem(1)[0],
        scratch_shapes=list(scratch),
        compiler_params=pltpu.CompilerParams(vmem_limit_bytes=8 * 1024 * 1024),
        cost_estimate=cost,
        interpret=INTERPRET,
    )


def local(blended, estimate, neighbour_sources, partner_lags, threshold_level):
    own_lags = jnp.pad(jnp.concatenate([partner_lags[:, slot] for slot in range(6)]), (0, 32))
    own_lags = jnp.broadcast_to(own_lags, (DEVS, 128))
    all_lags = lax.all_to_all(own_lags, "shot", 0, 0, tiled=True)
    old = estimate.astype(jnp.float32)
    res, part, level = call(
        residual_kernel,
        [
            jax.ShapeDtypeStruct((36 * CHANS * 8, 128), jnp.float32),
            jax.ShapeDtypeStruct((192 * 8, 128), jnp.float32),
            jax.ShapeDtypeStruct((8, 128), jnp.float32),
        ],
        [smem()] + vmem(3),
        [
            pltpu.VMEM((20 * CHANS * STEP + 16, 128), jnp.float32),
            pltpu.SMEM((128,), jnp.int32),
            pltpu.SemaphoreType.DMA,
        ],
        pl.CostEstimate(flops=4_000_000, bytes_accessed=16_000_000, transcendentals=0),
    )(threshold_level, own_lags, blended - old, old)
    rows = call(
        blend_kernel,
        jax.ShapeDtypeStruct((512, 512), jnp.bfloat16),
        vmem(3),
        [
            pltpu.VMEM((44 * CHANS * STEP + 16, 128), jnp.float32),
            pltpu.VMEM((2048, 128), jnp.float32),
            pltpu.SMEM((6, 128), jnp.int32),
            pltpu.SemaphoreType.DMA((6,)),
        ],
    )(all_lags, res, part)
    send = call(
        time_kernel,
        jax.ShapeDtypeStruct((DEVS * 24, 128), jnp.bfloat16),
        vmem(2),
        [pltpu.VMEM((DEVS // 2, 2, 24, 128), jnp.float32)],
    )(rows, time_table())
    columns = lax.all_to_all(send.reshape(DEVS, 24, 128), "shot", 0, 0, tiled=True).reshape(DEVS * 24, 128)
    others = lax.axis_size("chan")
    spec, limit = call(
        forward_kernel,
        [jax.ShapeDtypeStruct((512, 128), jnp.float32), jax.ShapeDtypeStruct((others, 128), jnp.float32)],
        vmem(5),
        [pltpu.VMEM((512, 128), jnp.float32)],
    )(level, columns, place_table(), twiddles(), block_table(-1))
    limits = lax.all_to_all(limit, "chan", 0, 0, tiled=True)
    back = call(
        backward_kernel,
        jax.ShapeDtypeStruct((512, 128), jnp.bfloat16),
        vmem(5),
        [pltpu.VMEM((512, 128), jnp.float32)],
    )(spec, limits, place_table(), twiddles(), block_table(1))
    arrived = lax.all_to_all(back.reshape(DEVS, 8, 128), "shot", 0, 0, tiled=True).reshape(512, 128)
    return call(
        time_back_kernel,
        jax.ShapeDtypeStruct((BLOCK, CHANS, SAMPLES), jnp.float32),
        vmem(2),
    )(arrived, time_back_table())


def solution(mesh):
    shots = P("shot", "chan", None)
    return jax.shard_map(
        local,
        mesh=mesh,
        in_specs=(shots, shots, P("shot", None), P("shot", None), P()),
        out_specs=shots,
        check_vma=False,
    )
```
